256 devices in a mesh: block: 16 (over x, y), replica: 16 (over z, core).
Axes of the slice: x: 4, y: 4, z: 8, core: 2. Of those that a mesh axis runs over, the one named last changes fastest.
Arguments:
- public_grads: float32 [512, 524288], P(None, ('block', 'replica')), may hold values from -32 to 32
- private_grads: float32 [256, 524288], P('replica', 'block'), may hold values from -100 to 100
- slot: int32 [256], replicated, may hold values from 0 to 255, each once
- seed_basis: int32 [512, 256], replicated, may hold values from -3 to 3
Outputs:
- basis: float32 [524288, 256], P(('block', 'replica'))
- public_coords: float32 [512, 256], replicated
- embeddings: float32 [256, 256], replicated
- residuals: float32 [256, 524288], P(None, ('block', 'replica'))
The draws below stay inside these ranges and needn't reach their ends.
Inputs may be any that keep to these rules, and one draw needn't show every extreme that they name: slot is a permutation of the private examples.
All inputs are finite; a program needn't handle non-finite values.
Results may differ from the reference program's by a relative error of at most 0.000096.
Values sent between devices are 32-bit elements; how exact they have to be, the bound alone decides.
No kernel may reach another device: no remote copies, remote signals or barrier semaphores. Data moves between devices by JAX's collectives and lax.ppermute only.
A program may use at most 64 MiB of HBM per device.

```python
import jax
import jax.numpy as jnp
from jax import lax

M = 512
K = 256
B = 256
PARAMS = 524288


def shared_parts(key):
    base_key, col_key = jax.random.split(key)
    common = jnp.clip(jax.random.normal(base_key, (M, PARAMS), jnp.float32), -4.0, 4.0)
    place = jnp.arange(PARAMS, dtype=jnp.float32) / PARAMS
    rough = jax.random.uniform(col_key, (PARAMS,), jnp.float32, 0.7, 1.3)
    col_scale = jnp.exp(jnp.log(3.0) * place) * rough
    return (common, col_scale)


def draw_public_grads(key, part):
    common, col_scale = shared_parts(key)
    key = jax.random.fold_in(key, 11)
    row_scale = jnp.exp(jax.random.uniform(key, (M, 1), jnp.float32, jnp.log(0.5), jnp.log(2.0)))
    return common * row_scale * col_scale[None, :]


def draw_private_grads(key, part):
    common, col_scale = shared_parts(key)
    key = jax.random.fold_in(key, 23)
    noise_key, scale_key = jax.random.split(key)
    noise = jnp.clip(jax.random.normal(noise_key, (B, PARAMS), jnp.float32), -4.0, 4.0)
    row_scale = jnp.exp(jax.random.uniform(scale_key, (B, 1), jnp.float32, jnp.log(0.25), jnp.log(4.0)))
    return row_scale * (common[:B] + 0.6 * noise) * col_scale[None, :]


def place_ends(entries, stream_key, smallest, largest):
    longest = entries.shape.index(max(entries.shape))
    spots = []
    for shift in (0, 1):
        where = [jax.random.randint(jax.random.fold_in(stream_key, axis), (), 0, length) for axis, length in enumerate(entries.shape)]
        where[longest] = (where[longest] + shift) % entries.shape[longest]
        spots.append(tuple(where))
    return entries.at[spots[0]].set(smallest).at[spots[1]].set(largest)


def setup_inputs(seed: int = 0) -> dict:
    seeds = jax.random.split(jax.random.key(seed), 5)
    public_grads = draw_public_grads(jax.random.fold_in(seeds[4], 71), 0)
    private_grads = draw_private_grads(jax.random.fold_in(seeds[4], 71), 0)
    slot = jax.random.permutation(seeds[2], B).astype(jnp.int32)
    seed_basis = place_ends(jax.random.randint(seeds[3], (M, K), -3, 4), jax.random.fold_in(seeds[3], 1), -3, 3).astype(jnp.int32)
    return dict(public_grads=public_grads, private_grads=private_grads, slot=slot, seed_basis=seed_basis)


HIGH = lax.Precision.HIGHEST

def cholesky_qr(tall, count):
    gram = lax.dot_general(tall, tall, (((0,), (0,)), ((), ())), precision=HIGH) / count
    lower = jnp.linalg.cholesky(gram)
    return lax.linalg.triangular_solve(lower, tall, left_side=False, lower=True, transpose_a=True)

def clip_rows(matrix, bound):
    size = jnp.sqrt(lax.optimization_barrier(jnp.sum(matrix * matrix, axis=1, keepdims=True)) + 1e-06)
    return matrix * jnp.minimum(1.0, bound / size)

def reference(public_grads, private_grads, slot, seed_basis):
    count = jnp.float32(PARAMS)
    start = seed_basis.astype(jnp.float32)
    first = lax.dot_general(public_grads, start, (((0,), (0,)), ((), ())), precision=HIGH)
    q_first = cholesky_qr(first, count)
    image = jnp.dot(public_grads, q_first, precision=HIGH) / count
    second = lax.dot_general(public_grads, image, (((0,), (0,)), ((), ())), precision=HIGH)
    basis = cholesky_qr(second, count)
    ordered = jnp.take(private_grads, slot, axis=0)
    root = jnp.sqrt(count)
    embed = jnp.dot(ordered, basis, precision=HIGH) / root
    resid = ordered - jnp.dot(embed, basis.T, precision=HIGH) / root
    embeddings = clip_rows(embed, 1.5 * jnp.sqrt(jnp.float32(K)))
    residuals = clip_rows(resid, 1.5 * root)
    return (basis, image, embeddings, residuals)
```

```python
import jax
import jax.numpy as jnp
from jax import lax
from jax.sharding import Mesh, PartitionSpec as P

K = 256
TILE = 128
HIGH = lax.Precision.HIGHEST
ALL = ("x", "y", "z", "core")
PLANE = ("x", "y", "core")


def mm(left, right, dims):
    return lax.dot_general(left, right, (dims, ((), ())), precision=HIGH, preferred_element_type=jnp.float32)


def exchange(pieces, axes):
    return lax.all_to_all(pieces, axes, split_axis=0, concat_axis=0, tiled=True)


def reduce_all(pieces):
    plane = lax.axis_size(PLANE)
    depth = lax.axis_size("z")
    mine = jnp.sum(exchange(pieces, PLANE), axis=0)
    total = jnp.sum(exchange(jnp.broadcast_to(mine[None], (depth,) + mine.shape), "z"), axis=0)
    return exchange(jnp.broadcast_to(total[None], (plane,) + total.shape), PLANE)


def pack_lower(gram):
    side = gram.shape[0] // TILE
    cells = [gram[i * TILE:(i + 1) * TILE, j * TILE:(j + 1) * TILE] for i in range(side) for j in range(i + 1)]
    return jnp.concatenate(cells, axis=0)


def unpack_lower(packed, side):
    cells = {}
    for i in range(side):
        for j in range(i + 1):
            at = (i * (i + 1) // 2 + j) * TILE
            cells[i, j] = packed[at:at + TILE]
    rows = [jnp.concatenate([cells[i, j] if j <= i else cells[j, i].T for j in range(side)], axis=1) for i in range(side)]
    return jnp.concatenate(rows, axis=0)


def inverse_lower(lower):
    return lax.linalg.triangular_solve(lower, jnp.eye(K, dtype=jnp.float32), left_side=True, lower=True)


def subspace(gram, start, count):
    image = mm(gram, start, ((1,), (0,)))
    gram_one = mm(start, image, ((0,), (0,))) / count
    inv_one = inverse_lower(jnp.linalg.cholesky(gram_one))
    coords = mm(image, inv_one, ((1,), (1,))) / count
    second = mm(gram, coords, ((1,), (0,)))
    gram_two = mm(coords, second, ((0,), (0,))) / count
    inv_two = inverse_lower(jnp.linalg.cholesky(gram_two))
    return coords, mm(coords, inv_two, ((1,), (1,)))


def body(public_grads, private_grads, slot, seed_basis):
    count = jnp.float32(public_grads.shape[1] * lax.axis_size(ALL))
    root = jnp.sqrt(count)
    rows = public_grads.shape[0]
    plane = lax.axis_size(PLANE)
    received = lax.all_to_all(private_grads, ("z", "core"), split_axis=1, concat_axis=0, tiled=True)
    packed = pack_lower(mm(public_grads, public_grads, ((1,), (1,))))
    packed = reduce_all(packed.reshape(plane, -1, TILE)).reshape(-1, TILE)
    gram = unpack_lower(packed, rows // TILE)
    coords, mix = subspace(gram, seed_basis.astype(jnp.float32), count)
    ordered = jnp.take(received, slot, axis=0)
    cross = mm(ordered, public_grads, ((1,), (1,)))
    norms = jnp.sum(ordered * ordered, axis=1, keepdims=True)
    joined = jnp.concatenate([cross, jnp.broadcast_to(norms, (norms.shape[0], TILE))], axis=1)
    joined = reduce_all(joined.reshape(plane, -1, joined.shape[1])).reshape(joined.shape)
    norms = joined[:, rows]
    embed = mm(joined[:, :rows], mix, ((1,), (0,))) / root
    basis = mm(public_grads, mix, ((0,), (0,)))
    resid = ordered - mm(embed, basis, ((1,), (1,))) / root
    embed_squares = jnp.sum(embed * embed, axis=1)
    resid_squares = jnp.maximum(norms - embed_squares, 0.0)
    bound = 1.5 * root
    close = (resid_squares < 0.02 * norms) & (norms > bound * bound)

    def exact(resid, rough):
        return lax.psum(jnp.sum(resid * resid, axis=1), ALL)

    def quick(resid, rough):
        return rough

    resid_squares = lax.cond(jnp.any(close), exact, quick, resid, resid_squares)
    embed_scale = jnp.minimum(1.0, 1.5 * jnp.sqrt(jnp.float32(K)) / jnp.sqrt(embed_squares + 1e-06))
    resid_scale = jnp.minimum(1.0, bound / jnp.sqrt(resid_squares + 1e-06))
    return (basis, coords, embed * embed_scale[:, None], resid * resid_scale[:, None])


def solution(mesh):
    fine = Mesh(mesh.devices.reshape(4, 4, 8, 2), ALL)
    return jax.shard_map(
        body,
        mesh=fine,
        in_specs=(P(None, ALL), P(("z", "core"), ("x", "y")), P(), P()),
        out_specs=(P(ALL, None), P(), P(), P(None, ALL)),
        check_vma=False,
    )
```

```python
import functools

import jax
import jax.numpy as jnp
from jax import lax
from jax.experimental import pallas as pl
from jax.experimental.pallas import tpu as pltpu
from jax.sharding import Mesh, PartitionSpec as P

K = 256
TILE = 128
NB = 32
STEP = 8
HIGH = lax.Precision.HIGHEST
ALL = ("x", "y", "z", "core")
PLANE = ("x", "y", "core")


def mm(left, right, dims):
    return lax.dot_general(left, right, (dims, ((), ())), precision=HIGH, preferred_element_type=jnp.float32)


def exchange(pieces, axes):
    return lax.all_to_all(pieces, axes, split_axis=0, concat_axis=0, tiled=True)


def reduce_all(pieces):
    plane = lax.axis_size(PLANE)
    depth = lax.axis_size("z")
    mine = jnp.sum(exchange(pieces, PLANE), axis=0)
    total = jnp.sum(exchange(jnp.broadcast_to(mine[None], (depth,) + mine.shape), "z"), axis=0)
    return exchange(jnp.broadcast_to(total[None], (plane,) + total.shape), PLANE)


def pack_lower(gram):
    side = gram.shape[0] // TILE
    cells = [gram[i * TILE:(i + 1) * TILE, j * TILE:(j + 1) * TILE] for i in range(side) for j in range(i + 1)]
    return jnp.concatenate(cells, axis=0)


def unpack_lower(packed, side):
    cells = {}
    for i in range(side):
        for j in range(i + 1):
            at = (i * (i + 1) // 2 + j) * TILE
            cells[i, j] = packed[at:at + TILE]
    rows = [jnp.concatenate([cells[i, j] if j <= i else cells[j, i].T for j in range(side)], axis=1) for i in range(side)]
    return jnp.concatenate(rows, axis=0)


def factor_block(diag):
    eye = (lax.broadcasted_iota(jnp.int32, (NB, NB), 0) == lax.broadcasted_iota(jnp.int32, (NB, NB), 1)).astype(jnp.float32)
    pad = jnp.zeros((NB, 128 - 2 * NB), jnp.float32)
    work = jnp.concatenate([diag, eye, pad], axis=1)
    row = lax.broadcasted_iota(jnp.int32, (NB, 128), 0)
    scale = jnp.zeros((NB, 128), jnp.float32)
    for j in range(0, NB, STEP):
        cols = [jnp.broadcast_to(work[:, j + c:j + c + 1], (NB, 128)) for c in range(STEP)]
        rows = [work[j + c:j + c + 1, :] for c in range(STEP)]
        piv = {(r, c): cols[c][j + r:j + r + 1, :] for r in range(STEP) for c in range(r + 1)}
        for c in range(STEP):
            inv = 1.0 / piv[c, c]
            low = {r: piv[r, c] * inv for r in range(c + 1, STEP)}
            for r in range(c + 1, STEP):
                for q in range(c + 1, r + 1):
                    piv[r, q] = piv[r, q] - low[r] * piv[q, c]
            for r in range(c + 1, STEP):
                rows[r] = rows[r] - low[r] * rows[c]
                cols[r] = cols[r] - low[r] * cols[c]
            scale = jnp.where(row == j + c, inv, scale)
            work = work - jnp.where(row > j + c, cols[c] * inv, 0.0) * rows[c]
    return (work * jnp.sqrt(scale))[:, NB:2 * NB]

def inverse_factor(gram, work):
    n = gram.shape[0]
    eye = (lax.broadcasted_iota(jnp.int32, (n, n), 0) == lax.broadcasted_iota(jnp.int32, (n, n), 1)).astype(jnp.float32)
    work[:, :n] = gram
    work[:, n:] = eye
    for b in range(0, n, NB):
        e = b + NB
        small = factor_block(work[b:e, b:e])
        lo = b // 128 * 128
        hi = n + (e + 127) // 128 * 128
        band = mm(small, work[b:e, lo:hi], ((1,), (0,)))
        work[b:e, lo:hi] = band
        if e < n:
            work[e:, lo:hi] = work[e:, lo:hi] - mm(band[:, e - lo:n - lo], band, ((0,), (0,)))
    return work[:, n:]

def subspace_kernel(count, gram_ref, start_ref, coords_ref, mix_ref, work):
    start = start_ref[...].astype(jnp.float32)
    image = mm(gram_ref[...], start, ((1,), (0,)))
    inv_one = inverse_factor(mm(start, image, ((0,), (0,))) * (1 / count), work)
    coords = mm(image, inv_one, ((1,), (1,))) * (1 / count)
    coords_ref[...] = coords
    second = mm(gram_ref[...], coords, ((1,), (0,)))
    inv_two = inverse_factor(mm(coords, second, ((0,), (0,))) * (1 / count), work)
    mix_ref[...] = mm(coords, inv_two, ((1,), (1,)))

def subspace(gram, start, count):
    shape = jax.ShapeDtypeStruct(start.shape, jnp.float32)
    return pl.pallas_call(
        functools.partial(subspace_kernel, count),
        out_shape=(shape, shape),
        in_specs=[pl.BlockSpec(memory_space=pltpu.VMEM)] * 2,
        out_specs=[pl.BlockSpec(memory_space=pltpu.VMEM)] * 2,
        scratch_shapes=[pltpu.VMEM((K, 2 * K), jnp.float32)],
        compiler_params=pltpu.CompilerParams(vmem_limit_bytes=32 * 1024 * 1024),
    )(gram, start)


def body(public_grads, private_grads, slot, seed_basis):
    count = jnp.float32(public_grads.shape[1] * lax.axis_size(ALL))
    root = jnp.sqrt(count)
    rows = public_grads.shape[0]
    plane = lax.axis_size(PLANE)
    received = lax.all_to_all(private_grads, ("z", "core"), split_axis=1, concat_axis=0, tiled=True)
    packed = pack_lower(mm(public_grads, public_grads, ((1,), (1,))))
    packed = reduce_all(packed.reshape(plane, -1, TILE)).reshape(-1, TILE)
    gram = unpack_lower(packed, rows // TILE)
    coords, mix = subspace(gram, seed_basis, float(public_grads.shape[1] * lax.axis_size(ALL)))
    ordered = jnp.take(received, slot, axis=0)
    cross = mm(ordered, public_grads, ((1,), (1,)))
    norms = jnp.sum(ordered * ordered, axis=1, keepdims=True)
    joined = jnp.concatenate([cross, jnp.broadcast_to(norms, (norms.shape[0], TILE))], axis=1)
    joined = reduce_all(joined.reshape(plane, -1, joined.shape[1])).reshape(joined.shape)
    norms = joined[:, rows]
    embed = mm(joined[:, :rows], mix, ((1,), (0,))) / root
    basis = mm(public_grads, mix, ((0,), (0,)))
    resid = ordered - mm(embed, basis, ((1,), (1,))) / root
    embed_squares = jnp.sum(embed * embed, axis=1)
    resid_squares = jnp.maximum(norms - embed_squares, 0.0)
    bound = 1.5 * root
    close = (resid_squares < 0.02 * norms) & (norms > bound * bound)

    def exact(resid, rough):
        return lax.psum(jnp.sum(resid * resid, axis=1), ALL)

    def quick(resid, rough):
        return rough

    resid_squares = lax.cond(jnp.any(close), exact, quick, resid, resid_squares)
    embed_scale = jnp.minimum(1.0, 1.5 * jnp.sqrt(jnp.float32(K)) / jnp.sqrt(embed_squares + 1e-06))
    resid_scale = jnp.minimum(1.0, bound / jnp.sqrt(resid_squares + 1e-06))
    return (basis, coords, embed * embed_scale[:, None], resid * resid_scale[:, None])


def solution(mesh):
    fine = Mesh(mesh.devices.reshape(4, 4, 8, 2), ALL)
    return jax.shard_map(
        body,
        mesh=fine,
        in_specs=(P(None, ALL), P(("z", "core"), ("x", "y")), P(), P()),
        out_specs=(P(ALL, None), P(), P(), P(None, ALL)),
        check_vma=False,
    )
```

```python
import functools

import jax
import jax.numpy as jnp
from jax import lax
from jax.experimental import pallas as pl
from jax.experimental.pallas import tpu as pltpu
from jax.sharding import Mesh, PartitionSpec as P

K = 256
TILE = 128
NB = 32
STEP = 8
HIGH = lax.Precision.HIGHEST
ALL = ("x", "y", "z", "core")
PLANE = ("x", "y", "core")


def mm(left, right, dims):
    return lax.dot_general(left, right, (dims, ((), ())), precision=HIGH, preferred_element_type=jnp.float32)


VMEM_LIMIT = 40 * 1024 * 1024


def in_vmem(count):
    return [pl.BlockSpec(memory_space=pltpu.VMEM)] * count


def exchange(pieces, axes):
    return lax.all_to_all(pieces, axes, split_axis=0, concat_axis=0, tiled=True)


def sum_kernel(pieces_ref, *refs):
    out_ref = refs[-1]
    out_ref[...] = jnp.broadcast_to(jnp.sum(pieces_ref[...], axis=0, keepdims=True), out_ref.shape)


def sum_and_copy(pieces, copies, after):
    return pl.pallas_call(
        sum_kernel,
        out_shape=jax.ShapeDtypeStruct((copies,) + pieces.shape[1:], jnp.float32),
        in_specs=in_vmem(1) + [pl.BlockSpec(memory_space=pl.ANY)] * len(after),
        out_specs=in_vmem(1)[0],
        compiler_params=pltpu.CompilerParams(vmem_limit_bytes=VMEM_LIMIT),
    )(pieces, *after)


def halves(value):
    high = value.astype(jnp.bfloat16)
    return high, (value - high.astype(jnp.float32)).astype(jnp.bfloat16)


def dot_low(left, right, dims):
    return lax.dot_general(left, right, (dims, ((), ())), preferred_element_type=jnp.float32)


def mm_halves(left, right, dims):
    small = dot_low(left[0], right[1], dims) + dot_low(left[1], right[0], dims)
    return dot_low(left[0], right[0], dims) + small


def cell_at(i, j):
    return (i * (i + 1) // 2 + j) * TILE


def gram_kernel(grads_ref, packed_ref):
    rows = grads_ref.shape[0]
    band = 2 * TILE
    first = pl.program_id(0) == 0
    high, low = halves(grads_ref[...])
    for top in range(0, rows, band):
        end = top + band
        part = mm_halves((high[top:end], low[top:end]), (high[:end], low[:end]), ((1,), (1,)))
        for i in (top // TILE, top // TILE + 1):
            for j in range(i + 1):
                at = cell_at(i, j)
                cell = part[i * TILE - top:(i + 1) * TILE - top, j * TILE:(j + 1) * TILE]
                packed_ref[at:at + TILE, :] = cell + jnp.where(first, 0.0, packed_ref[at:at + TILE, :])


def packed_gram(grads):
    rows, cols = grads.shape
    side = rows // TILE
    chunk = 512
    return pl.pallas_call(
        gram_kernel,
        grid=(cols // chunk,),
        out_shape=jax.ShapeDtypeStruct((side * (side + 1) // 2 * TILE, TILE), jnp.float32),
        in_specs=[pl.BlockSpec((rows, chunk), lambda i: (0, i))],
        out_specs=pl.BlockSpec((side * (side + 1) // 2 * TILE, TILE), lambda i: (0, 0)),
        compiler_params=pltpu.CompilerParams(vmem_limit_bytes=VMEM_LIMIT),
    )(grads)


def cross_kernel(parts, index_ref, grads_ref, *refs):
    held = [ref[...] for ref in refs[:parts]]
    joined_ref, ordered_ref = refs[parts + 1:]
    rows = grads_ref.shape[0]
    values = jnp.concatenate(held, axis=0)
    count = values.shape[0]
    pick = (index_ref[...] == lax.broadcasted_iota(jnp.int32, (count, count), 1)).astype(jnp.bfloat16)
    high, rest = values.astype(jnp.bfloat16), None
    rest = values - high.astype(jnp.float32)
    middle = rest.astype(jnp.bfloat16)
    low = (rest - middle.astype(jnp.float32)).astype(jnp.bfloat16)
    high, middle, low = [dot_low(pick, piece, ((1,), (0,))) for piece in (high, middle, low)]
    ordered = (high + middle) + low
    ordered_ref[...] = ordered
    left = (high.astype(jnp.bfloat16), middle.astype(jnp.bfloat16))
    joined_ref[:, :rows] = mm_halves(left, halves(grads_ref[...]), ((1,), (1,)))
    norms = jnp.sum(ordered * ordered, axis=1, keepdims=True)
    joined_ref[:, rows:] = jnp.broadcast_to(norms, (count, TILE))


def cross_products(index, grads, pieces, after):
    count = sum(piece.shape[0] for piece in pieces)
    rows, cols = grads.shape
    return pl.pallas_call(
        functools.partial(cross_kernel, len(pieces)),
        out_shape=(jax.ShapeDtypeStruct((count, rows + TILE), jnp.float32), jax.ShapeDtypeStruct((count, cols), jnp.float32)),
        in_specs=in_vmem(2 + len(pieces)) + [pl.BlockSpec(memory_space=pl.ANY)],
        out_specs=in_vmem(2),
        compiler_params=pltpu.CompilerParams(vmem_limit_bytes=VMEM_LIMIT),
    )(index, grads, *pieces, after)


def rows_kernel(root, joined_ref, mix_ref, out_ref):
    rows = mix_ref.shape[0]
    joined = jnp.sum(joined_ref[...], axis=0)
    embed = mm(joined[:, :rows], mix_ref[...], ((1,), (0,))) * (1 / root)
    held = jnp.concatenate([embed, joined[:, rows:]], axis=1)
    out_ref[...] = jnp.broadcast_to(held[None], out_ref.shape)


def embed_rows(joined, mix, copies, root):
    return pl.pallas_call(
        functools.partial(rows_kernel, root),
        out_shape=jax.ShapeDtypeStruct((copies, joined.shape[1], K + TILE), jnp.float32),
        in_specs=in_vmem(2),
        out_specs=in_vmem(1)[0],
        compiler_params=pltpu.CompilerParams(vmem_limit_bytes=VMEM_LIMIT),
    )(joined, mix)


def clip_kernel(root, held_ref, embed_ref, squares_ref, close_ref):
    embed = held_ref[:, :K]
    norms = held_ref[:, K:]
    squares = jnp.sum(embed * embed, axis=1, keepdims=True)
    embed_ref[...] = embed * jnp.minimum(1.0, 1.5 * K ** 0.5 / jnp.sqrt(squares + 1e-06))
    rough = jnp.maximum(norms - squares, 0.0)
    squares_ref[...] = rough
    close = (rough < 0.05 * norms) & (norms > 2.25 * root * root)
    close_ref[0, 0] = jnp.max(close.astype(jnp.int32))


def clip_embeddings(held, root):
    count = held.shape[0]
    return pl.pallas_call(
        functools.partial(clip_kernel, root),
        out_shape=(
            jax.ShapeDtypeStruct((count, K), jnp.float32),
            jax.ShapeDtypeStruct((count, TILE), jnp.float32),
            jax.ShapeDtypeStruct((1, 1), jnp.int32),
        ),
        in_specs=in_vmem(1),
        out_specs=in_vmem(2) + [pl.BlockSpec(memory_space=pltpu.SMEM)],
        compiler_params=pltpu.CompilerParams(vmem_limit_bytes=VMEM_LIMIT),
    )(held)


def final_kernel(root, ordered_ref, held_ref, squares_ref, basis_ref, out_ref):
    projected = mm_halves(halves(held_ref[:, :K]), halves(basis_ref[...]), ((1,), (1,)))
    scale = jnp.minimum(1.0, 1.5 * root / jnp.sqrt(squares_ref[:, :1] + 1e-06))
    out_ref[...] = (ordered_ref[...] - projected * (1 / root)) * scale


def scaled_residual(ordered, held, squares, basis, root):
    count, cols = ordered.shape
    chunk = 512
    return pl.pallas_call(
        functools.partial(final_kernel, root),
        grid=(cols // chunk,),
        out_shape=jax.ShapeDtypeStruct((count, cols), jnp.float32),
        in_specs=[
            pl.BlockSpec((count, chunk), lambda i: (0, i)),
            pl.BlockSpec((count, K + TILE), lambda i: (0, 0)),
            pl.BlockSpec((count, TILE), lambda i: (0, 0)),
            pl.BlockSpec((chunk, K), lambda i: (i, 0)),
        ],
        out_specs=pl.BlockSpec((count, chunk), lambda i: (0, i)),
        compiler_params=pltpu.CompilerParams(vmem_limit_bytes=VMEM_LIMIT),
    )(ordered, held, squares, basis)


def factor_block(diag):
    eye = (lax.broadcasted_iota(jnp.int32, (NB, NB), 0) == lax.broadcasted_iota(jnp.int32, (NB, NB), 1)).astype(jnp.float32)
    pad = jnp.zeros((NB, 128 - 2 * NB), jnp.float32)
    work = jnp.concatenate([diag, eye, pad], axis=1)
    row = lax.broadcasted_iota(jnp.int32, (NB, 128), 0)
    scale = jnp.zeros((NB, 128), jnp.float32)
    for j in range(0, NB, STEP):
        cols = [jnp.broadcast_to(work[:, j + c:j + c + 1], (NB, 128)) for c in range(STEP)]
        rows = [work[j + c:j + c + 1, :] for c in range(STEP)]
        piv = {(r, c): cols[c][j + r:j + r + 1, :] for r in range(STEP) for c in range(r + 1)}
        for c in range(STEP):
            inv = 1.0 / piv[c, c]
            low = {r: piv[r, c] * inv for r in range(c + 1, STEP)}
            for r in range(c + 1, STEP):
                for q in range(c + 1, r + 1):
                    piv[r, q] = piv[r, q] - low[r] * piv[q, c]
            for r in range(c + 1, STEP):
                rows[r] = rows[r] - low[r] * rows[c]
                cols[r] = cols[r] - low[r] * cols[c]
            scale = jnp.where(row == j + c, inv, scale)
            work = work - jnp.where(row > j + c, cols[c] * inv, 0.0) * rows[c]
    return (work * jnp.sqrt(scale))[:, NB:2 * NB]

def inverse_factor(gram, work):
    n = gram.shape[0]
    eye = (lax.broadcasted_iota(jnp.int32, (n, n), 0) == lax.broadcasted_iota(jnp.int32, (n, n), 1)).astype(jnp.float32)
    work[:, :n] = gram
    work[:, n:] = eye
    for b in range(0, n, NB):
        e = b + NB
        small = factor_block(work[b:e, b:e])
        lo = b // 128 * 128
        hi = n + (e + 127) // 128 * 128
        band = mm(small, work[b:e, lo:hi], ((1,), (0,)))
        work[b:e, lo:hi] = band
        if e < n:
            work[e:, lo:hi] = work[e:, lo:hi] - mm(band[:, e - lo:n - lo], band, ((0,), (0,)))
    return work[:, n:]

def first_kernel(count, packed_ref, start_ref, coords_ref, gram, work):
    side = start_ref.shape[0] // TILE
    for i in range(side):
        for j in range(i + 1):
            cell = packed_ref[cell_at(i, j):cell_at(i, j) + TILE, :]
            gram[i * TILE:(i + 1) * TILE, j * TILE:(j + 1) * TILE] = cell
            if j < i:
                gram[j * TILE:(j + 1) * TILE, i * TILE:(i + 1) * TILE] = cell.T
    start = start_ref[...].astype(jnp.float32)
    image = mm(gram[...], start, ((1,), (0,)))
    inv_one = inverse_factor(mm(start, image, ((0,), (0,))) * (1 / count), work)
    coords_ref[...] = mm(image, inv_one, ((1,), (1,))) * (1 / count)


def second_kernel(count, gram_ref, coords_ref, mix_ref, work):
    coords = coords_ref[...]
    image = mm(gram_ref[...], coords, ((1,), (0,)))
    inv_two = inverse_factor(mm(coords, image, ((0,), (0,))) * (1 / count), work)
    mix_ref[...] = mm(coords, inv_two, ((1,), (1,)))


def first_iterate(packed, start, count):
    rows = start.shape[0]
    return pl.pallas_call(
        functools.partial(first_kernel, count),
        out_shape=(jax.ShapeDtypeStruct(start.shape, jnp.float32), jax.ShapeDtypeStruct((rows, rows), jnp.float32)),
        in_specs=in_vmem(2),
        out_specs=in_vmem(2),
        scratch_shapes=[pltpu.VMEM((K, 2 * K), jnp.float32)],
        compiler_params=pltpu.CompilerParams(vmem_limit_bytes=VMEM_LIMIT),
    )(packed, start)


def second_iterate(gram, coords, count):
    return pl.pallas_call(
        functools.partial(second_kernel, count),
        out_shape=jax.ShapeDtypeStruct(coords.shape, jnp.float32),
        in_specs=in_vmem(2),
        out_specs=in_vmem(1)[0],
        scratch_shapes=[pltpu.VMEM((K, 2 * K), jnp.float32)],
        compiler_params=pltpu.CompilerParams(vmem_limit_bytes=VMEM_LIMIT),
    )(gram, coords)


def pair_rows(private_grads, cols):
    depth, pair = lax.axis_size("z"), lax.axis_size("core")
    core = lax.axis_index("core")
    local = private_grads.shape[0]
    blocks = private_grads.reshape(local, depth, pair, cols).transpose(1, 2, 0, 3)
    keep = lax.dynamic_index_in_dim(blocks, core, axis=1, keepdims=False)
    give = lax.dynamic_index_in_dim(blocks, 1 - core, axis=1, keepdims=False)
    got = lax.ppermute(give, "core", [(0, 1), (1, 0)])
    return jnp.concatenate([keep, got], axis=1)


def shifted(both, steps):
    depth, here = lax.axis_size("z"), lax.axis_index("z")
    pieces = []
    for step in steps:
        piece = lax.dynamic_index_in_dim(both, (here + step) % depth, axis=0, keepdims=False)
        if step:
            piece = lax.ppermute(piece, "z", [(i, (i + step) % depth) for i in range(depth)])
        pieces.append(piece)
    return pieces


def row_places(slot, local):
    depth, pair = lax.axis_size("z"), lax.axis_size("core")
    here, core = lax.axis_index("z"), lax.axis_index("core")
    owner = slot // local
    away = (here - owner // pair) % depth
    other = (owner % pair != core).astype(jnp.int32)
    return (away * pair + other) * local + slot % local


def body(public_grads, private_grads, slot, seed_basis):
    total = float(public_grads.shape[1] * lax.axis_size(ALL))
    root = total ** 0.5
    cols = public_grads.shape[1]
    plane, depth = lax.axis_size(PLANE), lax.axis_size("z")
    both = pair_rows(private_grads, cols)
    near, middle, far = [shifted(both, steps) for steps in ((1, depth - 1, 2, depth - 2), (3, depth - 3), (4,))]
    packed = packed_gram(public_grads)
    packed = exchange(packed.reshape(plane, -1, TILE), PLANE)
    packed = exchange(sum_and_copy(packed, depth, near), "z")
    packed = exchange(sum_and_copy(packed, plane, middle), PLANE).reshape(-1, TILE)
    places = row_places(slot, private_grads.shape[0])[:, None]
    here = shifted(both, (0,))
    pieces = [here[0], near[0], near[2], middle[0], far[0], middle[1], near[3], near[1]]
    joined, ordered = cross_products(places, public_grads, pieces, packed)
    joined = exchange(joined.reshape(plane, -1, joined.shape[1]), PLANE)
    coords, gram = first_iterate(packed, seed_basis, total)
    joined = exchange(sum_and_copy(joined, depth, [coords]), "z")
    mix = second_iterate(gram, coords, total)
    held = embed_rows(joined, mix, plane, root)
    held = exchange(held, PLANE).reshape(-1, held.shape[-1])
    basis = lax.dot_general(public_grads, mix, (((0,), (0,)), ((), ())), precision=lax.Precision.HIGH)
    embeddings, squares, close = clip_embeddings(held, root)

    def exact(rough):
        resid = ordered - mm(held[:, :K], basis, ((1,), (1,))) / root
        summed = lax.psum(jnp.sum(resid * resid, axis=1, keepdims=True), ALL)
        return jnp.broadcast_to(summed, rough.shape)

    def quick(rough):
        return rough

    squares = lax.cond(close[0, 0] > 0, exact, quick, squares)
    return (basis, coords, embeddings, scaled_residual(ordered, held, squares, basis, root))


def solution(mesh):
    fine = Mesh(mesh.devices.reshape(4, 4, 8, 2), ALL)
    return jax.shard_map(
        body,
        mesh=fine,
        in_specs=(P(None, ALL), P(("z", "core"), ("x", "y")), P(), P()),
        out_specs=(P(ALL, None), P(), P(), P(None, ALL)),
        check_vma=False,
    )
```

```python
import functools

import jax
import jax.numpy as jnp
from jax import lax
from jax.experimental import pallas as pl
from jax.experimental.pallas import tpu as pltpu
from jax.sharding import Mesh, PartitionSpec as P

K = 256
TILE = 128
NB = 32
STEP = 8
HIGH = lax.Precision.HIGHEST
ALL = ("x", "y", "z", "core")
PLANE = ("x", "y", "core")


def mm(left, right, dims):
    return lax.dot_general(left, right, (dims, ((), ())), precision=HIGH, preferred_element_type=jnp.float32)


VMEM_LIMIT = 40 * 1024 * 1024


def in_vmem(count):
    return [pl.BlockSpec(memory_space=pltpu.VMEM)] * count


def exchange(pieces, axes):
    return lax.all_to_all(pieces, axes, split_axis=0, concat_axis=0, tiled=True)


def sum_kernel(pieces_ref, *refs):
    out_ref = refs[-1]
    out_ref[...] = jnp.broadcast_to(jnp.sum(pieces_ref[...], axis=0, keepdims=True), out_ref.shape)


def sum_and_copy(pieces, copies, after):
    return pl.pallas_call(
        sum_kernel,
        out_shape=jax.ShapeDtypeStruct((copies,) + pieces.shape[1:], jnp.float32),
        in_specs=in_vmem(1) + [pl.BlockSpec(memory_space=pl.ANY)] * len(after),
        out_specs=in_vmem(1)[0],
        compiler_params=pltpu.CompilerParams(vmem_limit_bytes=VMEM_LIMIT),
    )(pieces, *after)


def halves(value):
    high = value.astype(jnp.bfloat16)
    return high, (value - high.astype(jnp.float32)).astype(jnp.bfloat16)


def dot_low(left, right, dims):
    return lax.dot_general(left, right, (dims, ((), ())), preferred_element_type=jnp.float32)


def mm_halves(left, right, dims):
    small = dot_low(left[0], right[1], dims) + dot_low(left[1], right[0], dims)
    return dot_low(left[0], right[0], dims) + small


def cell_at(i, j):
    return (i * (i + 1) // 2 + j) * TILE


def gram_kernel(grads_ref, packed_ref):
    rows = grads_ref.shape[0]
    band = 2 * TILE
    first = pl.program_id(0) == 0
    high, low = halves(grads_ref[...])
    for top in range(0, rows, band):
        end = top + band
        part = mm_halves((high[top:end], low[top:end]), (high[:end], low[:end]), ((1,), (1,)))
        for i in (top // TILE, top // TILE + 1):
            for j in range(i + 1):
                at = cell_at(i, j)
                cell = part[i * TILE - top:(i + 1) * TILE - top, j * TILE:(j + 1) * TILE]
                packed_ref[at:at + TILE, :] = cell + jnp.where(first, 0.0, packed_ref[at:at + TILE, :])


def packed_gram(grads):
    rows, cols = grads.shape
    side = rows // TILE
    chunk = 512
    return pl.pallas_call(
        gram_kernel,
        grid=(cols // chunk,),
        out_shape=jax.ShapeDtypeStruct((side * (side + 1) // 2 * TILE, TILE), jnp.float32),
        in_specs=[pl.BlockSpec((rows, chunk), lambda i: (0, i))],
        out_specs=pl.BlockSpec((side * (side + 1) // 2 * TILE, TILE), lambda i: (0, 0)),
        compiler_params=pltpu.CompilerParams(vmem_limit_bytes=VMEM_LIMIT),
    )(grads)


def cross_kernel(parts, index_ref, grads_ref, *refs):
    held = [ref[...] for ref in refs[:parts]]
    joined_ref, ordered_ref = refs[parts + 1:]
    rows = grads_ref.shape[0]
    values = jnp.concatenate(held, axis=0)
    count = values.shape[0]
    pick = (index_ref[...] == lax.broadcasted_iota(jnp.int32, (count, count), 1)).astype(jnp.bfloat16)
    high, rest = values.astype(jnp.bfloat16), None
    rest = values - high.astype(jnp.float32)
    middle = rest.astype(jnp.bfloat16)
    low = (rest - middle.astype(jnp.float32)).astype(jnp.bfloat16)
    high, middle, low = [dot_low(pick, piece, ((1,), (0,))) for piece in (high, middle, low)]
    ordered = (high + middle) + low
    ordered_ref[...] = ordered
    left = (high.astype(jnp.bfloat16), middle.astype(jnp.bfloat16))
    joined_ref[:, :rows] = mm_halves(left, halves(grads_ref[...]), ((1,), (1,)))
    norms = jnp.sum(ordered * ordered, axis=1, keepdims=True)
    joined_ref[:, rows:] = jnp.broadcast_to(norms, (count, TILE))


def cross_products(index, grads, pieces, after):
    count = sum(piece.shape[0] for piece in pieces)
    rows, cols = grads.shape
    return pl.pallas_call(
        functools.partial(cross_kernel, len(pieces)),
        out_shape=(jax.ShapeDtypeStruct((count, rows + TILE), jnp.float32), jax.ShapeDtypeStruct((count, cols), jnp.float32)),
        in_specs=in_vmem(2 + len(pieces)) + [pl.BlockSpec(memory_space=pl.ANY)],
        out_specs=in_vmem(2),
        compiler_params=pltpu.CompilerParams(vmem_limit_bytes=VMEM_LIMIT),
    )(index, grads, *pieces, after)


def rows_kernel(root, joined_ref, mix_ref, out_ref):
    rows = mix_ref.shape[0]
    joined = jnp.sum(joined_ref[...], axis=0)
    embed = mm(joined[:, :rows], mix_ref[...], ((1,), (0,))) * (1 / root)
    held = jnp.concatenate([embed, joined[:, rows:]], axis=1)
    out_ref[...] = jnp.broadcast_to(held[None], out_ref.shape)


def embed_rows(joined, mix, copies, root):
    return pl.pallas_call(
        functools.partial(rows_kernel, root),
        out_shape=jax.ShapeDtypeStruct((copies, joined.shape[1], K + TILE), jnp.float32),
        in_specs=in_vmem(2),
        out_specs=in_vmem(1)[0],
        compiler_params=pltpu.CompilerParams(vmem_limit_bytes=VMEM_LIMIT),
    )(joined, mix)


def clip_kernel(root, held_ref, embed_ref, squares_ref, close_ref):
    embed = held_ref[:, :K]
    norms = held_ref[:, K:]
    squares = jnp.sum(embed * embed, axis=1, keepdims=True)
    embed_ref[...] = embed * jnp.minimum(1.0, 1.5 * K ** 0.5 / jnp.sqrt(squares + 1e-06))
    rough = jnp.maximum(norms - squares, 0.0)
    squares_ref[...] = rough
    close = (rough < 0.05 * norms) & (norms > 2.25 * root * root)
    close_ref[0, 0] = jnp.max(close.astype(jnp.int32))


def clip_embeddings(held, root):
    count = held.shape[0]
    return pl.pallas_call(
        functools.partial(clip_kernel, root),
        out_shape=(
            jax.ShapeDtypeStruct((count, K), jnp.float32),
            jax.ShapeDtypeStruct((count, TILE), jnp.float32),
            jax.ShapeDtypeStruct((1, 1), jnp.int32),
        ),
        in_specs=in_vmem(1),
        out_specs=in_vmem(2) + [pl.BlockSpec(memory_space=pltpu.SMEM)],
        compiler_params=pltpu.CompilerParams(vmem_limit_bytes=VMEM_LIMIT),
    )(held)


def final_kernel(root, ordered_ref, held_ref, squares_ref, basis_ref, out_ref):
    projected = mm_halves(halves(held_ref[:, :K]), halves(basis_ref[...]), ((1,), (1,)))
    scale = jnp.minimum(1.0, 1.5 * root / jnp.sqrt(squares_ref[:, :1] + 1e-06))
    out_ref[...] = (ordered_ref[...] - projected * (1 / root)) * scale


def scaled_residual(ordered, held, squares, basis, root):
    count, cols = ordered.shape
    chunk = 512
    return pl.pallas_call(
        functools.partial(final_kernel, root),
        grid=(cols // chunk,),
        out_shape=jax.ShapeDtypeStruct((count, cols), jnp.float32),
        in_specs=[
            pl.BlockSpec((count, chunk), lambda i: (0, i)),
            pl.BlockSpec((count, K + TILE), lambda i: (0, 0)),
            pl.BlockSpec((count, TILE), lambda i: (0, 0)),
            pl.BlockSpec((chunk, K), lambda i: (i, 0)),
        ],
        out_specs=pl.BlockSpec((count, chunk), lambda i: (0, i)),
        compiler_params=pltpu.CompilerParams(vmem_limit_bytes=VMEM_LIMIT),
    )(ordered, held, squares, basis)


def factor_block(diag):
    eye = (lax.broadcasted_iota(jnp.int32, (NB, NB), 0) == lax.broadcasted_iota(jnp.int32, (NB, NB), 1)).astype(jnp.float32)
    pad = jnp.zeros((NB, 128 - 2 * NB), jnp.float32)
    work = jnp.concatenate([diag, eye, pad], axis=1)
    row = lax.broadcasted_iota(jnp.int32, (NB, 128), 0)
    scale = jnp.zeros((NB, 128), jnp.float32)
    for j in range(0, NB, STEP):
        cols = [jnp.broadcast_to(work[:, j + c:j + c + 1], (NB, 128)) for c in range(STEP)]
        rows = [work[j + c:j + c + 1, :] for c in range(STEP)]
        piv = {(r, c): cols[c][j + r:j + r + 1, :] for r in range(STEP) for c in range(r + 1)}
        for c in range(STEP):
            inv = 1.0 / piv[c, c]
            low = {r: piv[r, c] * inv for r in range(c + 1, STEP)}
            for r in range(c + 1, STEP):
                for q in range(c + 1, r + 1):
                    piv[r, q] = piv[r, q] - low[r] * piv[q, c]
            for r in range(c + 1, STEP):
                rows[r] = rows[r] - low[r] * rows[c]
                cols[r] = cols[r] - low[r] * cols[c]
            scale = jnp.where(row == j + c, inv, scale)
            work = work - jnp.where(row > j + c, cols[c] * inv, 0.0) * rows[c]
    return (work * jnp.sqrt(scale))[:, NB:2 * NB]

def inverse_factor(gram, work):
    n = gram.shape[0]
    eye = (lax.broadcasted_iota(jnp.int32, (n, n), 0) == lax.broadcasted_iota(jnp.int32, (n, n), 1)).astype(jnp.float32)
    work[:, :n] = gram
    work[:, n:] = eye
    for b in range(0, n, NB):
        e = b + NB
        small = factor_block(work[b:e, b:e])
        lo = b // 128 * 128
        hi = n + (e + 127) // 128 * 128
        band = mm(small, work[b:e, lo:hi], ((1,), (0,)))
        work[b:e, lo:hi] = band
        if e < n:
            work[e:, lo:hi] = work[e:, lo:hi] - mm(band[:, e - lo:n - lo], band, ((0,), (0,)))
    return work[:, n:]

def first_kernel(count, packed_ref, start_ref, *refs):
    coords_ref, gram, work = refs[-3:]
    side = start_ref.shape[0] // TILE
    for i in range(side):
        for j in range(i + 1):
            cell = packed_ref[cell_at(i, j):cell_at(i, j) + TILE, :]
            gram[i * TILE:(i + 1) * TILE, j * TILE:(j + 1) * TILE] = cell
            if j < i:
                gram[j * TILE:(j + 1) * TILE, i * TILE:(i + 1) * TILE] = cell.T
    start = start_ref[...].astype(jnp.float32)
    image = mm(gram[...], start, ((1,), (0,)))
    inv_one = inverse_factor(mm(start, image, ((0,), (0,))) * (1 / count), work)
    coords_ref[...] = mm(image, inv_one, ((1,), (1,))) * (1 / count)


def second_kernel(count, gram_ref, coords_ref, mix_ref, work):
    coords = coords_ref[...]
    image = mm(gram_ref[...], coords, ((1,), (0,)))
    inv_two = inverse_factor(mm(coords, image, ((0,), (0,))) * (1 / count), work)
    mix_ref[...] = mm(coords, inv_two, ((1,), (1,)))


def first_iterate(packed, start, count, after):
    rows = start.shape[0]
    return pl.pallas_call(
        functools.partial(first_kernel, count),
        out_shape=(jax.ShapeDtypeStruct(start.shape, jnp.float32), jax.ShapeDtypeStruct((rows, rows), jnp.float32)),
        in_specs=in_vmem(2) + [pl.BlockSpec(memory_space=pl.ANY)] * len(after),
        out_specs=in_vmem(2),
        scratch_shapes=[pltpu.VMEM((K, 2 * K), jnp.float32)],
        compiler_params=pltpu.CompilerParams(vmem_limit_bytes=VMEM_LIMIT),
    )(packed, start, *after)


def second_iterate(gram, coords, count):
    return pl.pallas_call(
        functools.partial(second_kernel, count),
        out_shape=jax.ShapeDtypeStruct(coords.shape, jnp.float32),
        in_specs=in_vmem(2),
        out_specs=in_vmem(1)[0],
        scratch_shapes=[pltpu.VMEM((K, 2 * K), jnp.float32)],
        compiler_params=pltpu.CompilerParams(vmem_limit_bytes=VMEM_LIMIT),
    )(gram, coords)


def split_kernel(core_ref, private_ref, keep_ref, give_ref, sems):
    depth, _, cols = keep_ref.shape
    copies = []
    for at in range(depth):
        for side, target in enumerate((give_ref, keep_ref)):
            whose = core_ref[0] if side else 1 - core_ref[0]
            start = pl.multiple_of((2 * at + whose) * cols, cols)
            copy = pltpu.make_async_copy(private_ref.at[:, pl.ds(start, cols)], target.at[at], sems.at[2 * at + side])
            copy.start()
            copies.append(copy)
    for copy in copies:
        copy.wait()


def split_by_core(private_grads, cols):
    depth = lax.axis_size("z")
    shape = jax.ShapeDtypeStruct((depth, private_grads.shape[0], cols), jnp.float32)
    return pl.pallas_call(
        split_kernel,
        out_shape=(shape, shape),
        in_specs=[pl.BlockSpec(memory_space=pltpu.SMEM), pl.BlockSpec(memory_space=pl.ANY)],
        out_specs=[pl.BlockSpec(memory_space=pl.ANY)] * 2,
        scratch_shapes=[pltpu.SemaphoreType.DMA((2 * depth,))],
        compiler_params=pltpu.CompilerParams(vmem_limit_bytes=VMEM_LIMIT),
    )(lax.axis_index("core").astype(jnp.int32)[None], private_grads)


def shift(piece, step):
    depth = lax.axis_size("z")
    return lax.ppermute(piece, "z", [(i, (i + step) % depth) for i in range(depth)])


def row_places(slot, local):
    depth, pair = lax.axis_size("z"), lax.axis_size("core")
    here, core = lax.axis_index("z"), lax.axis_index("core")
    owner = slot // local
    away = (here - owner // pair) % depth
    other = (owner % pair != core).astype(jnp.int32)
    return (away * pair + other) * local + slot % local


def body(public_grads, private_grads, slot, seed_basis):
    total = float(public_grads.shape[1] * lax.axis_size(ALL))
    root = total ** 0.5
    cols = public_grads.shape[1]
    local = private_grads.shape[0]
    plane, depth = lax.axis_size(PLANE), lax.axis_size("z")
    here = lax.axis_index("z")
    keep, give = split_by_core(private_grads, cols)
    packed = packed_gram(public_grads)
    got = lax.ppermute(give, "core", [(0, 1), (1, 0)])

    def part(held, step):
        return lax.dynamic_index_in_dim(held, (here + step) % depth, axis=0, keepdims=False)

    def both(step):
        return jnp.concatenate([part(keep, step), part(got, step)], axis=0)

    pieces = {0: both(0)}
    pieces[2], pieces[6] = shift(both(2), 2), shift(both(6), 6)
    packed = exchange(packed.reshape(plane, -1, TILE), PLANE)
    packed = exchange(sum_and_copy(packed, depth, [pieces[2], pieces[6]]), "z")
    pieces[1], pieces[7] = shift(both(1), 1), shift(both(7), 7)
    relay = shift(part(got, 4), 6)
    packed = exchange(sum_and_copy(packed, plane, [pieces[1], pieces[7], relay]), PLANE).reshape(-1, TILE)
    far = [shift(part(keep, 4), 4), shift(relay, 6)]
    coords, gram = first_iterate(packed, seed_basis, total, far)
    pieces[3], pieces[5] = shift(both(3), 3), shift(both(5), 5)
    ordered_parts = [pieces[0], pieces[1], pieces[2], pieces[3], far[0], far[1], pieces[5], pieces[6], pieces[7]]
    places = row_places(slot, local)[:, None]
    joined, ordered = cross_products(places, public_grads, ordered_parts, coords)
    joined = exchange(joined.reshape(plane, -1, joined.shape[1]), PLANE)
    mix = second_iterate(gram, coords, total)
    joined = exchange(sum_and_copy(joined, depth, [mix]), "z")
    held = embed_rows(joined, mix, plane, root)
    held = exchange(held, PLANE).reshape(-1, held.shape[-1])
    basis = lax.dot_general(public_grads, mix, (((0,), (0,)), ((), ())), precision=lax.Precision.HIGH)
    embeddings, squares, close = clip_embeddings(held, root)

    def exact(rough):
        resid = ordered - mm(held[:, :K], basis, ((1,), (1,))) / root
        summed = lax.psum(jnp.sum(resid * resid, axis=1, keepdims=True), ALL)
        return jnp.broadcast_to(summed, rough.shape)

    def quick(rough):
        return rough

    squares = lax.cond(close[0, 0] > 0, exact, quick, squares)
    return (basis, coords, embeddings, scaled_residual(ordered, held, squares, basis, root))


def solution(mesh):
    fine = Mesh(mesh.devices.reshape(4, 4, 8, 2), ALL)
    return jax.shard_map(
        body,
        mesh=fine,
        in_specs=(P(None, ALL), P(("z", "core"), ("x", "y")), P(), P()),
        out_specs=(P(ALL, None), P(), P(), P(None, ALL)),
        check_vma=False,
    )
```

```python
import functools

import jax
import jax.numpy as jnp
from jax import lax
from jax.experimental import pallas as pl
from jax.experimental.pallas import tpu as pltpu
from jax.sharding import Mesh, PartitionSpec as P

K = 256
TILE = 128
NB = 32
STEP = 8
HIGH = lax.Precision.HIGHEST
ALL = ("x", "y", "z", "core")
PLANE = ("x", "y", "core")


def mm(left, right, dims):
    return lax.dot_general(left, right, (dims, ((), ())), precision=HIGH, preferred_element_type=jnp.float32)


VMEM_LIMIT = 40 * 1024 * 1024


def in_vmem(count):
    return [pl.BlockSpec(memory_space=pltpu.VMEM)] * count


def exchange(pieces, axes):
    return lax.all_to_all(pieces, axes, split_axis=0, concat_axis=0, tiled=True)


def sum_kernel(pieces_ref, *refs):
    out_ref = refs[-1]
    out_ref[...] = jnp.broadcast_to(jnp.sum(pieces_ref[...], axis=0, keepdims=True), out_ref.shape)


def sum_and_copy(pieces, copies, after):
    return pl.pallas_call(
        sum_kernel,
        out_shape=jax.ShapeDtypeStruct((copies,) + pieces.shape[1:], jnp.float32),
        in_specs=in_vmem(1) + [pl.BlockSpec(memory_space=pl.ANY)] * len(after),
        out_specs=in_vmem(1)[0],
        compiler_params=pltpu.CompilerParams(vmem_limit_bytes=VMEM_LIMIT),
    )(pieces, *after)


def halves(value):
    high = value.astype(jnp.bfloat16)
    return high, (value - high.astype(jnp.float32)).astype(jnp.bfloat16)


def dot_low(left, right, dims):
    return lax.dot_general(left, right, (dims, ((), ())), preferred_element_type=jnp.float32)


def mm_halves(left, right, dims):
    small = dot_low(left[0], right[1], dims) + dot_low(left[1], right[0], dims)
    return dot_low(left[0], right[0], dims) + small


def cell_at(i, j):
    return (i * (i + 1) // 2 + j) * TILE


def gram_kernel(grads_ref, packed_ref):
    rows = grads_ref.shape[0]
    band = 2 * TILE
    first = pl.program_id(0) == 0
    high, low = halves(grads_ref[...])
    for top in range(0, rows, band):
        end = top + band
        part = mm_halves((high[top:end], low[top:end]), (high[:end], low[:end]), ((1,), (1,)))
        for i in (top // TILE, top // TILE + 1):
            for j in range(i + 1):
                at = cell_at(i, j)
                cell = part[i * TILE - top:(i + 1) * TILE - top, j * TILE:(j + 1) * TILE]
                packed_ref[at:at + TILE, :] = cell + jnp.where(first, 0.0, packed_ref[at:at + TILE, :])


def packed_gram(grads):
    rows, cols = grads.shape
    side = rows // TILE
    chunk = 512
    return pl.pallas_call(
        gram_kernel,
        grid=(cols // chunk,),
        out_shape=jax.ShapeDtypeStruct((side * (side + 1) // 2 * TILE, TILE), jnp.float32),
        in_specs=[pl.BlockSpec((rows, chunk), lambda i: (0, i))],
        out_specs=pl.BlockSpec((side * (side + 1) // 2 * TILE, TILE), lambda i: (0, 0)),
        compiler_params=pltpu.CompilerParams(vmem_limit_bytes=VMEM_LIMIT),
    )(grads)


def cross_kernel(parts, index_ref, grads_ref, *refs):
    held = [ref[...] for ref in refs[:parts]]
    joined_ref, ordered_ref = refs[parts + 1:]
    rows = grads_ref.shape[0]
    values = jnp.concatenate(held, axis=0)
    count = values.shape[0]
    pick = (index_ref[...] == lax.broadcasted_iota(jnp.int32, (count, count), 1)).astype(jnp.bfloat16)
    high, rest = values.astype(jnp.bfloat16), None
    rest = values - high.astype(jnp.float32)
    middle = rest.astype(jnp.bfloat16)
    low = (rest - middle.astype(jnp.float32)).astype(jnp.bfloat16)
    high, middle, low = [dot_low(pick, piece, ((1,), (0,))) for piece in (high, middle, low)]
    ordered = (high + middle) + low
    ordered_ref[...] = ordered
    left = (high.astype(jnp.bfloat16), middle.astype(jnp.bfloat16))
    joined_ref[:, :rows] = mm_halves(left, halves(grads_ref[...]), ((1,), (1,)))
    norms = jnp.sum(ordered * ordered, axis=1, keepdims=True)
    joined_ref[:, rows:] = jnp.broadcast_to(norms, (count, TILE))


def cross_products(index, grads, pieces, after):
    count = sum(piece.shape[0] for piece in pieces)
    rows, cols = grads.shape
    return pl.pallas_call(
        functools.partial(cross_kernel, len(pieces)),
        out_shape=(jax.ShapeDtypeStruct((count, rows + TILE), jnp.float32), jax.ShapeDtypeStruct((count, cols), jnp.float32)),
        in_specs=in_vmem(2 + len(pieces)) + [pl.BlockSpec(memory_space=pl.ANY)],
        out_specs=in_vmem(2),
        compiler_params=pltpu.CompilerParams(vmem_limit_bytes=VMEM_LIMIT),
    )(index, grads, *pieces, after)


def rows_kernel(root, joined_ref, mix_ref, out_ref):
    rows = mix_ref.shape[0]
    joined = jnp.sum(joined_ref[...], axis=0)
    embed = mm(joined[:, :rows], mix_ref[...], ((1,), (0,))) * (1 / root)
    held = jnp.concatenate([embed, joined[:, rows:]], axis=1)
    out_ref[...] = jnp.broadcast_to(held[None], out_ref.shape)


def embed_rows(joined, mix, copies, root):
    return pl.pallas_call(
        functools.partial(rows_kernel, root),
        out_shape=jax.ShapeDtypeStruct((copies, joined.shape[1], K + TILE), jnp.float32),
        in_specs=in_vmem(2),
        out_specs=in_vmem(1)[0],
        compiler_params=pltpu.CompilerParams(vmem_limit_bytes=VMEM_LIMIT),
    )(joined, mix)


def clip_kernel(root, held_ref, embed_ref, squares_ref, close_ref):
    embed = held_ref[:, :K]
    norms = held_ref[:, K:]
    squares = jnp.sum(embed * embed, axis=1, keepdims=True)
    embed_ref[...] = embed * jnp.minimum(1.0, 1.5 * K ** 0.5 / jnp.sqrt(squares + 1e-06))
    rough = jnp.maximum(norms - squares, 0.0)
    squares_ref[...] = rough
    close = (rough < 0.05 * norms) & (norms > 2.25 * root * root)
    close_ref[0, 0] = jnp.max(close.astype(jnp.int32))


def clip_embeddings(held, root):
    count = held.shape[0]
    return pl.pallas_call(
        functools.partial(clip_kernel, root),
        out_shape=(
            jax.ShapeDtypeStruct((count, K), jnp.float32),
            jax.ShapeDtypeStruct((count, TILE), jnp.float32),
            jax.ShapeDtypeStruct((1, 1), jnp.int32),
        ),
        in_specs=in_vmem(1),
        out_specs=in_vmem(2) + [pl.BlockSpec(memory_space=pltpu.SMEM)],
        compiler_params=pltpu.CompilerParams(vmem_limit_bytes=VMEM_LIMIT),
    )(held)


def final_kernel(root, ordered_ref, held_ref, squares_ref, basis_ref, out_ref):
    projected = mm_halves(halves(held_ref[:, :K]), halves(basis_ref[...]), ((1,), (1,)))
    scale = jnp.minimum(1.0, 1.5 * root / jnp.sqrt(squares_ref[:, :1] + 1e-06))
    out_ref[...] = (ordered_ref[...] - projected * (1 / root)) * scale


def scaled_residual(ordered, held, squares, basis, root):
    count, cols = ordered.shape
    chunk = 512
    return pl.pallas_call(
        functools.partial(final_kernel, root),
        grid=(cols // chunk,),
        out_shape=jax.ShapeDtypeStruct((count, cols), jnp.float32),
        in_specs=[
            pl.BlockSpec((count, chunk), lambda i: (0, i)),
            pl.BlockSpec((count, K + TILE), lambda i: (0, 0)),
            pl.BlockSpec((count, TILE), lambda i: (0, 0)),
            pl.BlockSpec((chunk, K), lambda i: (i, 0)),
        ],
        out_specs=pl.BlockSpec((count, chunk), lambda i: (0, i)),
        compiler_params=pltpu.CompilerParams(vmem_limit_bytes=VMEM_LIMIT),
    )(ordered, held, squares, basis)


def factor_block(diag):
    eye = (lax.broadcasted_iota(jnp.int32, (NB, NB), 0) == lax.broadcasted_iota(jnp.int32, (NB, NB), 1)).astype(jnp.float32)
    pad = jnp.zeros((NB, 128 - 2 * NB), jnp.float32)
    work = jnp.concatenate([diag, eye, pad], axis=1)
    row = lax.broadcasted_iota(jnp.int32, (NB, 128), 0)
    scale = jnp.zeros((NB, 128), jnp.float32)
    for j in range(0, NB, STEP):
        cols = [jnp.broadcast_to(work[:, j + c:j + c + 1], (NB, 128)) for c in range(STEP)]
        rows = [work[j + c:j + c + 1, :] for c in range(STEP)]
        piv = {(r, c): cols[c][j + r:j + r + 1, :] for r in range(STEP) for c in range(r + 1)}
        for c in range(STEP):
            inv = 1.0 / piv[c, c]
            low = {r: piv[r, c] * inv for r in range(c + 1, STEP)}
            for r in range(c + 1, STEP):
                for q in range(c + 1, r + 1):
                    piv[r, q] = piv[r, q] - low[r] * piv[q, c]
            for r in range(c + 1, STEP):
                rows[r] = rows[r] - low[r] * rows[c]
                cols[r] = cols[r] - low[r] * cols[c]
            scale = jnp.where(row == j + c, inv, scale)
            work = work - jnp.where(row > j + c, cols[c] * inv, 0.0) * rows[c]
    return (work * jnp.sqrt(scale))[:, NB:2 * NB]

def inverse_factor(gram, work):
    n = gram.shape[0]
    eye = (lax.broadcasted_iota(jnp.int32, (n, n), 0) == lax.broadcasted_iota(jnp.int32, (n, n), 1)).astype(jnp.float32)
    work[:, :n] = gram
    work[:, n:] = eye
    for b in range(0, n, NB):
        e = b + NB
        small = factor_block(work[b:e, b:e])
        lo = b // 128 * 128
        hi = n + (e + 127) // 128 * 128
        band = mm(small, work[b:e, lo:hi], ((1,), (0,)))
        work[b:e, lo:hi] = band
        if e < n:
            work[e:, lo:hi] = work[e:, lo:hi] - mm(band[:, e - lo:n - lo], band, ((0,), (0,)))
    return work[:, n:]

def first_kernel(count, packed_ref, start_ref, *refs):
    coords_ref, gram, work = refs[-3:]
    side = start_ref.shape[0] // TILE
    for i in range(side):
        for j in range(i + 1):
            cell = packed_ref[cell_at(i, j):cell_at(i, j) + TILE, :]
            gram[i * TILE:(i + 1) * TILE, j * TILE:(j + 1) * TILE] = cell
            if j < i:
                gram[j * TILE:(j + 1) * TILE, i * TILE:(i + 1) * TILE] = cell.T
    start = start_ref[...].astype(jnp.float32)
    image = mm(gram[...], start, ((1,), (0,)))
    inv_one = inverse_factor(mm(start, image, ((0,), (0,))) * (1 / count), work)
    coords_ref[...] = mm(image, inv_one, ((1,), (1,))) * (1 / count)


def second_kernel(count, gram_ref, coords_ref, *refs):
    mix_ref, work = refs[-2:]
    coords = coords_ref[...]
    image = mm(gram_ref[...], coords, ((1,), (0,)))
    inv_two = inverse_factor(mm(coords, image, ((0,), (0,))) * (1 / count), work)
    mix_ref[...] = mm(coords, inv_two, ((1,), (1,)))


def first_iterate(packed, start, count, after):
    rows = start.shape[0]
    return pl.pallas_call(
        functools.partial(first_kernel, count),
        out_shape=(jax.ShapeDtypeStruct(start.shape, jnp.float32), jax.ShapeDtypeStruct((rows, rows), jnp.float32)),
        in_specs=in_vmem(2) + [pl.BlockSpec(memory_space=pl.ANY)] * len(after),
        out_specs=in_vmem(2),
        scratch_shapes=[pltpu.VMEM((K, 2 * K), jnp.float32)],
        compiler_params=pltpu.CompilerParams(vmem_limit_bytes=VMEM_LIMIT),
    )(packed, start, *after)


def second_iterate(gram, coords, count, after):
    return pl.pallas_call(
        functools.partial(second_kernel, count),
        out_shape=jax.ShapeDtypeStruct(coords.shape, jnp.float32),
        in_specs=in_vmem(2) + [pl.BlockSpec(memory_space=pl.ANY)] * len(after),
        out_specs=in_vmem(1)[0],
        scratch_shapes=[pltpu.VMEM((K, 2 * K), jnp.float32)],
        compiler_params=pltpu.CompilerParams(vmem_limit_bytes=VMEM_LIMIT),
    )(gram, coords, *after)


def split_kernel(core_ref, private_ref, keep_ref, give_ref, sems):
    depth, _, cols = keep_ref.shape
    copies = []
    for at in range(depth):
        for side, target in enumerate((give_ref, keep_ref)):
            whose = core_ref[0] if side else 1 - core_ref[0]
            start = pl.multiple_of((2 * at + whose) * cols, cols)
            copy = pltpu.make_async_copy(private_ref.at[:, pl.ds(start, cols)], target.at[at], sems.at[2 * at + side])
            copy.start()
            copies.append(copy)
    for copy in copies:
        copy.wait()


def split_by_core(private_grads, cols):
    depth = lax.axis_size("z")
    shape = jax.ShapeDtypeStruct((depth, private_grads.shape[0], cols), jnp.float32)
    return pl.pallas_call(
        split_kernel,
        out_shape=(shape, shape),
        in_specs=[pl.BlockSpec(memory_space=pltpu.SMEM), pl.BlockSpec(memory_space=pl.ANY)],
        out_specs=[pl.BlockSpec(memory_space=pl.ANY)] * 2,
        scratch_shapes=[pltpu.SemaphoreType.DMA((2 * depth,))],
        compiler_params=pltpu.CompilerParams(vmem_limit_bytes=VMEM_LIMIT),
    )(lax.axis_index("core").astype(jnp.int32)[None], private_grads)


def take_kernel(parts, place_ref, *refs):
    held, outs, sems = refs[:len(parts[0])], refs[-len(parts) - 1:-1], refs[-1]
    copies = []
    for at, (part, out_ref) in enumerate(zip(parts, outs)):
        rows = 0
        for which, ref in enumerate(held):
            if part[which]:
                target = out_ref.at[pl.ds(rows, ref.shape[1])]
                copy = pltpu.make_async_copy(ref.at[place_ref[at]], target, sems.at[len(copies)])
                copy.start()
                copies.append(copy)
                rows += ref.shape[1]
    for copy in copies:
        copy.wait()


def take_parts(keep, got, steps, parts, after):
    depth, here = lax.axis_size("z"), lax.axis_index("z")
    local, cols = keep.shape[1:]
    places = jnp.stack([(here + step) % depth for step in steps]).astype(jnp.int32)
    shapes = [jax.ShapeDtypeStruct((sum(part) * local, cols), jnp.float32) for part in parts]
    anywhere = pl.BlockSpec(memory_space=pl.ANY)
    return pl.pallas_call(
        functools.partial(take_kernel, parts),
        out_shape=shapes,
        in_specs=[pl.BlockSpec(memory_space=pltpu.SMEM)] + [anywhere] * (2 + len(after)),
        out_specs=[anywhere] * len(parts),
        scratch_shapes=[pltpu.SemaphoreType.DMA((sum(sum(part) for part in parts),))],
        compiler_params=pltpu.CompilerParams(vmem_limit_bytes=VMEM_LIMIT),
    )(places, keep, got, *after)


def shift(piece, step):
    depth = lax.axis_size("z")
    return lax.ppermute(piece, "z", [(i, (i + step) % depth) for i in range(depth)])


def row_places(slot, local):
    depth, pair = lax.axis_size("z"), lax.axis_size("core")
    here, core = lax.axis_index("z"), lax.axis_index("core")
    owner = slot // local
    away = (here - owner // pair) % depth
    other = (owner % pair != core).astype(jnp.int32)
    return (away * pair + other) * local + slot % local


def body(public_grads, private_grads, slot, seed_basis):
    total = float(public_grads.shape[1] * lax.axis_size(ALL))
    root = total ** 0.5
    cols = public_grads.shape[1]
    local = private_grads.shape[0]
    plane, depth = lax.axis_size(PLANE), lax.axis_size("z")
    keep, give = split_by_core(private_grads, cols)
    packed = packed_gram(public_grads)
    got = lax.ppermute(give, "core", [(0, 1), (1, 0)])
    whole, own, other = (1, 1), (1, 0), (0, 1)
    one, seven, half = take_parts(keep, got, (1, 7, 4), (whole, whole, other), [])
    one, seven = shift(one, 1), shift(seven, 7)
    packed = exchange(packed.reshape(plane, -1, TILE), PLANE)
    packed = sum_and_copy(packed, depth, [one, seven])
    relay = shift(half, 6)
    packed = exchange(packed, "z")
    packed = sum_and_copy(packed, plane, [relay])
    two, six, zero = take_parts(keep, got, (2, 6, 0), (whole, whole, whole), [packed])
    two, six = shift(two, 2), shift(six, 6)
    packed = exchange(packed, PLANE).reshape(-1, TILE)
    three, five = take_parts(keep, got, (3, 5), (whole, whole), [packed, two, six])
    three, five = shift(three, 3), shift(five, 5)
    coords, gram = first_iterate(packed, seed_basis, total, [two, six])
    (four,) = take_parts(keep, got, (4,), (own,), [coords])
    four, back = shift(four, 4), shift(relay, 6)
    mix = second_iterate(gram, coords, total, [three, five])
    ordered_parts = [zero, one, two, three, four, back, five, six, seven]
    places = row_places(slot, local)[:, None]
    joined, ordered = cross_products(places, public_grads, ordered_parts, mix)
    joined = exchange(joined.reshape(plane, -1, joined.shape[1]), PLANE)
    joined = exchange(sum_and_copy(joined, depth, []), "z")
    held = embed_rows(joined, mix, plane, root)
    held = exchange(held, PLANE).reshape(-1, held.shape[-1])
    basis = lax.dot_general(public_grads, mix, (((0,), (0,)), ((), ())), precision=lax.Precision.HIGH)
    embeddings, squares, close = clip_embeddings(held, root)

    def exact(rough):
        resid = ordered - mm(held[:, :K], basis, ((1,), (1,))) / root
        summed = lax.psum(jnp.sum(resid * resid, axis=1, keepdims=True), ALL)
        return jnp.broadcast_to(summed, rough.shape)

    def quick(rough):
        return rough

    squares = lax.cond(close[0, 0] > 0, exact, quick, squares)
    return (basis, coords, embeddings, scaled_residual(ordered, held, squares, basis, root))


def solution(mesh):
    fine = Mesh(mesh.devices.reshape(4, 4, 8, 2), ALL)
    return jax.shard_map(
        body,
        mesh=fine,
        in_specs=(P(None, ALL), P(("z", "core"), ("x", "y")), P(), P()),
        out_specs=(P(ALL, None), P(), P(), P(None, ALL)),
        check_vma=False,
    )
```

```python
import functools

import jax
import jax.numpy as jnp
from jax import lax
from jax.experimental import pallas as pl
from jax.experimental.pallas import tpu as pltpu
from jax.sharding import Mesh, PartitionSpec as P

K = 256
TILE = 128
NB = 32
STEP = 8
HIGH = lax.Precision.HIGHEST
ALL = ("x", "y", "z", "core")
PLANE = ("x", "y", "core")


def mm(left, right, dims):
    return lax.dot_general(left, right, (dims, ((), ())), precision=HIGH, preferred_element_type=jnp.float32)


VMEM_LIMIT = 40 * 1024 * 1024


def in_vmem(count):
    return [pl.BlockSpec(memory_space=pltpu.VMEM)] * count


def exchange(pieces, axes):
    return lax.all_to_all(pieces, axes, split_axis=0, concat_axis=0, tiled=True)


def sum_kernel(pieces_ref, *refs):
    out_ref = refs[-1]
    out_ref[...] = jnp.broadcast_to(jnp.sum(pieces_ref[...], axis=0, keepdims=True), out_ref.shape)


def sum_and_copy(pieces, copies, after):
    return pl.pallas_call(
        sum_kernel,
        out_shape=jax.ShapeDtypeStruct((copies,) + pieces.shape[1:], jnp.float32),
        in_specs=in_vmem(1) + [pl.BlockSpec(memory_space=pl.ANY)] * len(after),
        out_specs=in_vmem(1)[0],
        compiler_params=pltpu.CompilerParams(vmem_limit_bytes=VMEM_LIMIT),
    )(pieces, *after)


def halves(value):
    high = value.astype(jnp.bfloat16)
    return high, (value - high.astype(jnp.float32)).astype(jnp.bfloat16)


def dot_low(left, right, dims):
    return lax.dot_general(left, right, (dims, ((), ())), preferred_element_type=jnp.float32)


def mm_halves(left, right, dims):
    small = dot_low(left[0], right[1], dims) + dot_low(left[1], right[0], dims)
    return dot_low(left[0], right[0], dims) + small


def cell_at(i, j):
    return (i * (i + 1) // 2 + j) * TILE


def gram_kernel(grads_ref, packed_ref):
    rows = grads_ref.shape[0]
    band = 2 * TILE
    first = pl.program_id(0) == 0
    high, low = halves(grads_ref[...])
    for top in range(0, rows, band):
        end = top + band
        part = mm_halves((high[top:end], low[top:end]), (high[:end], low[:end]), ((1,), (1,)))
        for i in (top // TILE, top // TILE + 1):
            for j in range(i + 1):
                at = cell_at(i, j)
                cell = part[i * TILE - top:(i + 1) * TILE - top, j * TILE:(j + 1) * TILE]
                packed_ref[at:at + TILE, :] = cell + jnp.where(first, 0.0, packed_ref[at:at + TILE, :])


def packed_gram(grads):
    rows, cols = grads.shape
    side = rows // TILE
    chunk = 512
    return pl.pallas_call(
        gram_kernel,
        grid=(cols // chunk,),
        out_shape=jax.ShapeDtypeStruct((side * (side + 1) // 2 * TILE, TILE), jnp.float32),
        in_specs=[pl.BlockSpec((rows, chunk), lambda i: (0, i))],
        out_specs=pl.BlockSpec((side * (side + 1) // 2 * TILE, TILE), lambda i: (0, 0)),
        compiler_params=pltpu.CompilerParams(vmem_limit_bytes=VMEM_LIMIT),
    )(grads)


def cross_kernel(parts, index_ref, *refs):
    held, (joined_ref, ordered_ref, rows_ref, grads, sems) = refs[:parts + 1], refs[-5:]
    copies, at = [], 0
    for piece in held[:parts]:
        copies.append(pltpu.make_async_copy(piece, rows_ref.at[pl.ds(at, piece.shape[0])], sems.at[len(copies)]))
        at += piece.shape[0]
    copies.append(pltpu.make_async_copy(held[parts], grads, sems.at[parts]))
    for copy in copies:
        copy.start()
    for copy in copies[:parts]:
        copy.wait()
    rows = grads.shape[0]
    values = rows_ref[...]
    count = values.shape[0]
    pick = (index_ref[...] == lax.broadcasted_iota(jnp.int32, (count, count), 1)).astype(jnp.bfloat16)
    high = values.astype(jnp.bfloat16)
    rest = values - high.astype(jnp.float32)
    middle = rest.astype(jnp.bfloat16)
    low = (rest - middle.astype(jnp.float32)).astype(jnp.bfloat16)
    high, middle, low = [dot_low(pick, piece, ((1,), (0,))) for piece in (high, middle, low)]
    ordered = (high + middle) + low
    ordered_ref[...] = ordered
    norms = jnp.sum(ordered * ordered, axis=1, keepdims=True)
    joined_ref[:, rows:] = jnp.broadcast_to(norms, (count, TILE))
    left = (high.astype(jnp.bfloat16), middle.astype(jnp.bfloat16))
    copies[parts].wait()
    joined_ref[:, :rows] = mm_halves(left, halves(grads[...]), ((1,), (1,)))


def cross_products(index, grads, pieces, after):
    count = sum(piece.shape[0] for piece in pieces)
    rows, cols = grads.shape
    anywhere = pl.BlockSpec(memory_space=pl.ANY)
    return pl.pallas_call(
        functools.partial(cross_kernel, len(pieces)),
        out_shape=(jax.ShapeDtypeStruct((count, rows + TILE), jnp.float32), jax.ShapeDtypeStruct((count, cols), jnp.float32)),
        in_specs=in_vmem(1) + [anywhere] * (2 + len(pieces)),
        out_specs=in_vmem(2),
        scratch_shapes=[
            pltpu.VMEM((count, cols), jnp.float32),
            pltpu.VMEM((rows, cols), jnp.float32),
            pltpu.SemaphoreType.DMA((len(pieces) + 1,)),
        ],
        compiler_params=pltpu.CompilerParams(vmem_limit_bytes=VMEM_LIMIT),
    )(index, *pieces, grads, after)


def rows_kernel(root, joined_ref, mix_ref, out_ref):
    rows = mix_ref.shape[0]
    joined = jnp.sum(joined_ref[...], axis=0)
    embed = mm(joined[:, :rows], mix_ref[...], ((1,), (0,))) * (1 / root)
    held = jnp.concatenate([embed, joined[:, rows:]], axis=1)
    out_ref[...] = jnp.broadcast_to(held[None], out_ref.shape)


def embed_rows(joined, mix, copies, root):
    return pl.pallas_call(
        functools.partial(rows_kernel, root),
        out_shape=jax.ShapeDtypeStruct((copies, joined.shape[1], K + TILE), jnp.float32),
        in_specs=in_vmem(2),
        out_specs=in_vmem(1)[0],
        compiler_params=pltpu.CompilerParams(vmem_limit_bytes=VMEM_LIMIT),
    )(joined, mix)


def clip_kernel(root, held_ref, embed_ref, squares_ref, close_ref):
    embed = held_ref[:, :K]
    norms = held_ref[:, K:]
    squares = jnp.sum(embed * embed, axis=1, keepdims=True)
    embed_ref[...] = embed * jnp.minimum(1.0, 1.5 * K ** 0.5 / jnp.sqrt(squares + 1e-06))
    rough = jnp.maximum(norms - squares, 0.0)
    squares_ref[...] = rough
    close = (rough < 0.05 * norms) & (norms > 2.25 * root * root)
    close_ref[0, 0] = jnp.max(close.astype(jnp.int32))


def clip_embeddings(held, root):
    count = held.shape[0]
    return pl.pallas_call(
        functools.partial(clip_kernel, root),
        out_shape=(
            jax.ShapeDtypeStruct((count, K), jnp.float32),
            jax.ShapeDtypeStruct((count, TILE), jnp.float32),
            jax.ShapeDtypeStruct((1, 1), jnp.int32),
        ),
        in_specs=in_vmem(1),
        out_specs=in_vmem(2) + [pl.BlockSpec(memory_space=pltpu.SMEM)],
        compiler_params=pltpu.CompilerParams(vmem_limit_bytes=VMEM_LIMIT),
    )(held)


def final_kernel(root, ordered_ref, held_ref, squares_ref, basis_ref, out_ref):
    projected = mm_halves(halves(held_ref[:, :K]), halves(basis_ref[...]), ((1,), (1,)))
    scale = jnp.minimum(1.0, 1.5 * root / jnp.sqrt(squares_ref[:, :1] + 1e-06))
    out_ref[...] = (ordered_ref[...] - projected * (1 / root)) * scale


def scaled_residual(ordered, held, squares, basis, root):
    count, cols = ordered.shape
    chunk = 512
    return pl.pallas_call(
        functools.partial(final_kernel, root),
        grid=(cols // chunk,),
        out_shape=jax.ShapeDtypeStruct((count, cols), jnp.float32),
        in_specs=[
            pl.BlockSpec((count, chunk), lambda i: (0, i)),
            pl.BlockSpec((count, K + TILE), lambda i: (0, 0)),
            pl.BlockSpec((count, TILE), lambda i: (0, 0)),
            pl.BlockSpec((chunk, K), lambda i: (i, 0)),
        ],
        out_specs=pl.BlockSpec((count, chunk), lambda i: (0, i)),
        compiler_params=pltpu.CompilerParams(vmem_limit_bytes=VMEM_LIMIT),
    )(ordered, held, squares, basis)


def factor_block(diag):
    eye = (lax.broadcasted_iota(jnp.int32, (NB, NB), 0) == lax.broadcasted_iota(jnp.int32, (NB, NB), 1)).astype(jnp.float32)
    pad = jnp.zeros((NB, 128 - 2 * NB), jnp.float32)
    work = jnp.concatenate([diag, eye, pad], axis=1)
    row = lax.broadcasted_iota(jnp.int32, (NB, 128), 0)
    scale = jnp.zeros((NB, 128), jnp.float32)
    for j in range(0, NB, STEP):
        cols = [jnp.broadcast_to(work[:, j + c:j + c + 1], (NB, 128)) for c in range(STEP)]
        rows = [work[j + c:j + c + 1, :] for c in range(STEP)]
        piv = {(r, c): cols[c][j + r:j + r + 1, :] for r in range(STEP) for c in range(r + 1)}
        for c in range(STEP):
            inv = 1.0 / piv[c, c]
            low = {r: piv[r, c] * inv for r in range(c + 1, STEP)}
            for r in range(c + 1, STEP):
                for q in range(c + 1, r + 1):
                    piv[r, q] = piv[r, q] - low[r] * piv[q, c]
            for r in range(c + 1, STEP):
                rows[r] = rows[r] - low[r] * rows[c]
                cols[r] = cols[r] - low[r] * cols[c]
            scale = jnp.where(row == j + c, inv, scale)
            work = work - jnp.where(row > j + c, cols[c] * inv, 0.0) * rows[c]
    return (work * jnp.sqrt(scale))[:, NB:2 * NB]

def inverse_factor(gram, work):
    n = gram.shape[0]
    eye = (lax.broadcasted_iota(jnp.int32, (n, n), 0) == lax.broadcasted_iota(jnp.int32, (n, n), 1)).astype(jnp.float32)
    work[:, :n] = gram
    work[:, n:] = eye
    for b in range(0, n, NB):
        e = b + NB
        small = factor_block(work[b:e, b:e])
        lo = b // 128 * 128
        hi = n + (e + 127) // 128 * 128
        band = mm(small, work[b:e, lo:hi], ((1,), (0,)))
        work[b:e, lo:hi] = band
        if e < n:
            work[e:, lo:hi] = work[e:, lo:hi] - mm(band[:, e - lo:n - lo], band, ((0,), (0,)))
    return work[:, n:]

def first_kernel(count, packed_ref, start_ref, *refs):
    coords_ref, gram, work = refs[-3:]
    side = start_ref.shape[0] // TILE
    for i in range(side):
        for j in range(i + 1):
            cell = packed_ref[cell_at(i, j):cell_at(i, j) + TILE, :]
            gram[i * TILE:(i + 1) * TILE, j * TILE:(j + 1) * TILE] = cell
            if j < i:
                gram[j * TILE:(j + 1) * TILE, i * TILE:(i + 1) * TILE] = cell.T
    start = start_ref[...].astype(jnp.float32)
    image = mm(gram[...], start, ((1,), (0,)))
    inv_one = inverse_factor(mm(start, image, ((0,), (0,))) * (1 / count), work)
    coords_ref[...] = mm(image, inv_one, ((1,), (1,))) * (1 / count)


def second_kernel(count, gram_ref, coords_ref, *refs):
    mix_ref, work = refs[-2:]
    coords = coords_ref[...]
    image = mm(gram_ref[...], coords, ((1,), (0,)))
    inv_two = inverse_factor(mm(coords, image, ((0,), (0,))) * (1 / count), work)
    mix_ref[...] = mm(coords, inv_two, ((1,), (1,)))


def first_iterate(packed, start, count, after):
    rows = start.shape[0]
    return pl.pallas_call(
        functools.partial(first_kernel, count),
        out_shape=(jax.ShapeDtypeStruct(start.shape, jnp.float32), jax.ShapeDtypeStruct((rows, rows), jnp.float32)),
        in_specs=in_vmem(2) + [pl.BlockSpec(memory_space=pl.ANY)] * len(after),
        out_specs=in_vmem(2),
        scratch_shapes=[pltpu.VMEM((K, 2 * K), jnp.float32)],
        compiler_params=pltpu.CompilerParams(vmem_limit_bytes=VMEM_LIMIT),
    )(packed, start, *after)


def second_iterate(gram, coords, count, after):
    return pl.pallas_call(
        functools.partial(second_kernel, count),
        out_shape=jax.ShapeDtypeStruct(coords.shape, jnp.float32),
        in_specs=in_vmem(2) + [pl.BlockSpec(memory_space=pl.ANY)] * len(after),
        out_specs=in_vmem(1)[0],
        scratch_shapes=[pltpu.VMEM((K, 2 * K), jnp.float32)],
        compiler_params=pltpu.CompilerParams(vmem_limit_bytes=VMEM_LIMIT),
    )(gram, coords, *after)


def split_kernel(core_ref, private_ref, keep_ref, give_ref, sems):
    depth, _, cols = keep_ref.shape
    copies = []
    for at in range(depth):
        for side, target in enumerate((give_ref, keep_ref)):
            whose = core_ref[0] if side else 1 - core_ref[0]
            start = pl.multiple_of((2 * at + whose) * cols, cols)
            copy = pltpu.make_async_copy(private_ref.at[:, pl.ds(start, cols)], target.at[at], sems.at[2 * at + side])
            copy.start()
            copies.append(copy)
    for copy in copies:
        copy.wait()


def split_by_core(private_grads, cols):
    depth = lax.axis_size("z")
    shape = jax.ShapeDtypeStruct((depth, private_grads.shape[0], cols), jnp.float32)
    return pl.pallas_call(
        split_kernel,
        out_shape=(shape, shape),
        in_specs=[pl.BlockSpec(memory_space=pltpu.SMEM), pl.BlockSpec(memory_space=pl.ANY)],
        out_specs=[pl.BlockSpec(memory_space=pl.ANY)] * 2,
        scratch_shapes=[pltpu.SemaphoreType.DMA((2 * depth,))],
        compiler_params=pltpu.CompilerParams(vmem_limit_bytes=VMEM_LIMIT),
    )(lax.axis_index("core").astype(jnp.int32)[None], private_grads)


def take_kernel(parts, place_ref, *refs):
    held, outs, sems = refs[:len(parts[0])], refs[-len(parts) - 1:-1], refs[-1]
    copies = []
    for at, (part, out_ref) in enumerate(zip(parts, outs)):
        rows = 0
        for which, ref in enumerate(held):
            if part[which]:
                target = out_ref.at[pl.ds(rows, ref.shape[1])]
                copy = pltpu.make_async_copy(ref.at[place_ref[at]], target, sems.at[len(copies)])
                copy.start()
                copies.append(copy)
                rows += ref.shape[1]
    for copy in copies:
        copy.wait()


def take_parts(keep, got, steps, parts, after):
    depth, here = lax.axis_size("z"), lax.axis_index("z")
    local, cols = keep.shape[1:]
    places = jnp.stack([(here + step) % depth for step in steps]).astype(jnp.int32)
    shapes = [jax.ShapeDtypeStruct((sum(part) * local, cols), jnp.float32) for part in parts]
    anywhere = pl.BlockSpec(memory_space=pl.ANY)
    return pl.pallas_call(
        functools.partial(take_kernel, parts),
        out_shape=shapes,
        in_specs=[pl.BlockSpec(memory_space=pltpu.SMEM)] + [anywhere] * (2 + len(after)),
        out_specs=[anywhere] * len(parts),
        scratch_shapes=[pltpu.SemaphoreType.DMA((sum(sum(part) for part in parts),))],
        compiler_params=pltpu.CompilerParams(vmem_limit_bytes=VMEM_LIMIT),
    )(places, keep, got, *after)


def shift(piece, step):
    depth = lax.axis_size("z")
    return lax.ppermute(piece, "z", [(i, (i + step) % depth) for i in range(depth)])


def row_places(slot, local):
    depth, pair = lax.axis_size("z"), lax.axis_size("core")
    here, core = lax.axis_index("z"), lax.axis_index("core")
    owner = slot // local
    away = (here - owner // pair) % depth
    other = (owner % pair != core).astype(jnp.int32)
    return (away * pair + other) * local + slot % local


def body(public_grads, private_grads, slot, seed_basis):
    total = float(public_grads.shape[1] * lax.axis_size(ALL))
    root = total ** 0.5
    cols = public_grads.shape[1]
    local = private_grads.shape[0]
    plane, depth = lax.axis_size(PLANE), lax.axis_size("z")
    keep, give = split_by_core(private_grads, cols)
    packed = packed_gram(public_grads)
    got = lax.ppermute(give, "core", [(0, 1), (1, 0)])
    whole, own, other = (1, 1), (1, 0), (0, 1)
    zero, one, seven = take_parts(keep, got, (0, 1, 7), (whole, whole, whole), [])
    one, seven = shift(one, 1), shift(seven, 7)
    packed = exchange(packed.reshape(plane, -1, TILE), PLANE)
    packed = exchange(sum_and_copy(packed, depth, [one, seven]), "z")
    packed = sum_and_copy(packed, plane, [])
    steps, parts = (3, 5, 4, 4, 2, 6), (whole, whole, own, other, whole, whole)
    three, five, four, relay, two, six = take_parts(keep, got, steps, parts, [packed])
    three, five, four, relay = shift(three, 3), shift(five, 5), shift(four, 4), shift(relay, 6)
    two, six, back = shift(two, 2), shift(six, 6), shift(relay, 6)
    packed = exchange(packed, PLANE).reshape(-1, TILE)
    coords, gram = first_iterate(packed, seed_basis, total, [])
    ordered_parts = [zero, one, two, three, four, back, five, six, seven]
    places = row_places(slot, local)[:, None]
    joined, ordered = cross_products(places, public_grads, ordered_parts, coords)
    joined = exchange(joined.reshape(plane, -1, joined.shape[1]), PLANE)
    mix = second_iterate(gram, coords, total, [])
    joined = exchange(sum_and_copy(joined, depth, [mix]), "z")
    held = embed_rows(joined, mix, plane, root)
    held = exchange(held, PLANE).reshape(-1, held.shape[-1])
    basis = lax.dot_general(public_grads, mix, (((0,), (0,)), ((), ())), precision=lax.Precision.HIGH)
    embeddings, squares, close = clip_embeddings(held, root)

    def exact(rough):
        resid = ordered - mm(held[:, :K], basis, ((1,), (1,))) / root
        summed = lax.psum(jnp.sum(resid * resid, axis=1, keepdims=True), ALL)
        return jnp.broadcast_to(summed, rough.shape)

    def quick(rough):
        return rough

    squares = lax.cond(close[0, 0] > 0, exact, quick, squares)
    return (basis, coords, embeddings, scaled_residual(ordered, held, squares, basis, root))


def solution(mesh):
    fine = Mesh(mesh.devices.reshape(4, 4, 8, 2), ALL)
    return jax.shard_map(
        body,
        mesh=fine,
        in_specs=(P(None, ALL), P(("z", "core"), ("x", "y")), P(), P()),
        out_specs=(P(ALL, None), P(), P(), P(None, ALL)),
        check_vma=False,
    )
```

```python
import functools

import jax
import jax.numpy as jnp
from jax import lax
from jax.experimental import pallas as pl
from jax.experimental.pallas import tpu as pltpu
from jax.sharding import Mesh, PartitionSpec as P

K = 256
TILE = 128
NB = 32
STEP = 8
HIGH = lax.Precision.HIGHEST
ALL = ("x", "y", "z", "core")
PLANE = ("x", "y", "core")


def mm(left, right, dims):
    return lax.dot_general(left, right, (dims, ((), ())), precision=HIGH, preferred_element_type=jnp.float32)


MIB = 1024 * 1024


def in_vmem(count):
    return [pl.BlockSpec(memory_space=pltpu.VMEM)] * count


def exchange(pieces, axes):
    return lax.all_to_all(pieces, axes, split_axis=0, concat_axis=0, tiled=True)


def sum_kernel(pieces_ref, *refs):
    out_ref = refs[-1]
    out_ref[...] = jnp.broadcast_to(jnp.sum(pieces_ref[...], axis=0, keepdims=True), out_ref.shape)


def sum_and_copy(pieces, copies, after):
    return pl.pallas_call(
        sum_kernel,
        out_shape=jax.ShapeDtypeStruct((copies,) + pieces.shape[1:], jnp.float32),
        in_specs=in_vmem(1) + [pl.BlockSpec(memory_space=pl.ANY)] * len(after),
        out_specs=in_vmem(1)[0],
        compiler_params=pltpu.CompilerParams(vmem_limit_bytes=8 * MIB),
    )(pieces, *after)


def halves(value):
    high = value.astype(jnp.bfloat16)
    return high, (value - high.astype(jnp.float32)).astype(jnp.bfloat16)


def dot_low(left, right, dims):
    return lax.dot_general(left, right, (dims, ((), ())), preferred_element_type=jnp.float32)


def mm_halves(left, right, dims):
    small = dot_low(left[0], right[1], dims) + dot_low(left[1], right[0], dims)
    return dot_low(left[0], right[0], dims) + small


def cell_at(i, j):
    return (i * (i + 1) // 2 + j) * TILE


def gram_kernel(grads_ref, packed_ref):
    rows = grads_ref.shape[0]
    band = 2 * TILE
    first = pl.program_id(0) == 0
    high, low = halves(grads_ref[...])
    for top in range(0, rows, band):
        end = top + band
        part = mm_halves((high[top:end], low[top:end]), (high[:end], low[:end]), ((1,), (1,)))
        for i in (top // TILE, top // TILE + 1):
            for j in range(i + 1):
                at = cell_at(i, j)
                cell = part[i * TILE - top:(i + 1) * TILE - top, j * TILE:(j + 1) * TILE]
                packed_ref[at:at + TILE, :] = cell + jnp.where(first, 0.0, packed_ref[at:at + TILE, :])


def packed_gram(grads):
    rows, cols = grads.shape
    side = rows // TILE
    chunk = 512
    return pl.pallas_call(
        gram_kernel,
        grid=(cols // chunk,),
        out_shape=jax.ShapeDtypeStruct((side * (side + 1) // 2 * TILE, TILE), jnp.float32),
        in_specs=[pl.BlockSpec((rows, chunk), lambda i: (0, i))],
        out_specs=pl.BlockSpec((side * (side + 1) // 2 * TILE, TILE), lambda i: (0, 0)),
        compiler_params=pltpu.CompilerParams(vmem_limit_bytes=12 * MIB),
    )(grads)


def cross_kernel(parts, index_ref, *refs):
    held, (joined_ref, ordered_ref, rows_ref, grads, sems) = refs[:parts + 1], refs[-5:]
    copies, at = [], 0
    for piece in held[:parts]:
        copies.append(pltpu.make_async_copy(piece, rows_ref.at[pl.ds(at, piece.shape[0])], sems.at[len(copies)]))
        at += piece.shape[0]
    copies.append(pltpu.make_async_copy(held[parts], grads, sems.at[parts]))
    for copy in copies:
        copy.start()
    for copy in copies[:parts]:
        copy.wait()
    rows = grads.shape[0]
    values = rows_ref[...]
    count = values.shape[0]
    pick = (index_ref[...] == lax.broadcasted_iota(jnp.int32, (count, count), 1)).astype(jnp.bfloat16)
    high = values.astype(jnp.bfloat16)
    rest = values - high.astype(jnp.float32)
    middle = rest.astype(jnp.bfloat16)
    low = (rest - middle.astype(jnp.float32)).astype(jnp.bfloat16)
    high, middle, low = [dot_low(pick, piece, ((1,), (0,))) for piece in (high, middle, low)]
    ordered = (high + middle) + low
    ordered_ref[...] = ordered
    norms = jnp.sum(ordered * ordered, axis=1, keepdims=True)
    joined_ref[:, rows:] = jnp.broadcast_to(norms, (count, TILE))
    left = (high.astype(jnp.bfloat16), middle.astype(jnp.bfloat16))
    copies[parts].wait()
    joined_ref[:, :rows] = mm_halves(left, halves(grads[...]), ((1,), (1,)))


def cross_products(index, grads, pieces, after):
    count = sum(piece.shape[0] for piece in pieces)
    rows, cols = grads.shape
    far = pl.BlockSpec(memory_space=pltpu.HBM)
    return pl.pallas_call(
        functools.partial(cross_kernel, len(pieces)),
        out_shape=(jax.ShapeDtypeStruct((count, rows + TILE), jnp.float32), jax.ShapeDtypeStruct((count, cols), jnp.float32)),
        in_specs=in_vmem(1) + [far] * (1 + len(pieces)) + [pl.BlockSpec(memory_space=pl.ANY)],
        out_specs=in_vmem(2),
        scratch_shapes=[
            pltpu.VMEM((count, cols), jnp.float32),
            pltpu.VMEM((rows, cols), jnp.float32),
            pltpu.SemaphoreType.DMA((len(pieces) + 1,)),
        ],
        compiler_params=pltpu.CompilerParams(vmem_limit_bytes=26 * MIB),
    )(index, *pieces, grads, after)


def rows_kernel(root, joined_ref, mix_ref, out_ref):
    rows = mix_ref.shape[0]
    joined = jnp.sum(joined_ref[...], axis=0)
    embed = mm(joined[:, :rows], mix_ref[...], ((1,), (0,))) * (1 / root)
    held = jnp.concatenate([embed, joined[:, rows:]], axis=1)
    out_ref[...] = jnp.broadcast_to(held[None], out_ref.shape)


def embed_rows(joined, mix, copies, root):
    return pl.pallas_call(
        functools.partial(rows_kernel, root),
        out_shape=jax.ShapeDtypeStruct((copies, joined.shape[1], K + TILE), jnp.float32),
        in_specs=in_vmem(2),
        out_specs=in_vmem(1)[0],
        compiler_params=pltpu.CompilerParams(vmem_limit_bytes=8 * MIB),
    )(joined, mix)


def clip_kernel(root, held_ref, embed_ref, squares_ref, close_ref):
    embed = held_ref[:, :K]
    norms = held_ref[:, K:]
    squares = jnp.sum(embed * embed, axis=1, keepdims=True)
    embed_ref[...] = embed * jnp.minimum(1.0, 1.5 * K ** 0.5 / jnp.sqrt(squares + 1e-06))
    rough = jnp.maximum(norms - squares, 0.0)
    squares_ref[...] = rough
    close = (rough < 0.05 * norms) & (norms > 2.25 * root * root)
    close_ref[0, 0] = jnp.max(close.astype(jnp.int32))


def clip_embeddings(held, root):
    count = held.shape[0]
    return pl.pallas_call(
        functools.partial(clip_kernel, root),
        out_shape=(
            jax.ShapeDtypeStruct((count, K), jnp.float32),
            jax.ShapeDtypeStruct((count, TILE), jnp.float32),
            jax.ShapeDtypeStruct((1, 1), jnp.int32),
        ),
        in_specs=in_vmem(1),
        out_specs=in_vmem(2) + [pl.BlockSpec(memory_space=pltpu.SMEM)],
        compiler_params=pltpu.CompilerParams(vmem_limit_bytes=8 * MIB),
    )(held)


def final_kernel(root, ordered_ref, held_ref, squares_ref, basis_ref, out_ref):
    projected = mm_halves(halves(held_ref[:, :K]), halves(basis_ref[...]), ((1,), (1,)))
    scale = jnp.minimum(1.0, 1.5 * root / jnp.sqrt(squares_ref[:, :1] + 1e-06))
    out_ref[...] = (ordered_ref[...] - projected * (1 / root)) * scale


def scaled_residual(ordered, held, squares, basis, root):
    count, cols = ordered.shape
    chunk = 512
    return pl.pallas_call(
        functools.partial(final_kernel, root),
        grid=(cols // chunk,),
        out_shape=jax.ShapeDtypeStruct((count, cols), jnp.float32),
        in_specs=[
            pl.BlockSpec((count, chunk), lambda i: (0, i)),
            pl.BlockSpec((count, K + TILE), lambda i: (0, 0)),
            pl.BlockSpec((count, TILE), lambda i: (0, 0)),
            pl.BlockSpec((chunk, K), lambda i: (i, 0)),
        ],
        out_specs=pl.BlockSpec((count, chunk), lambda i: (0, i)),
        compiler_params=pltpu.CompilerParams(vmem_limit_bytes=12 * MIB),
    )(ordered, held, squares, basis)


def factor_block(diag):
    eye = (lax.broadcasted_iota(jnp.int32, (NB, NB), 0) == lax.broadcasted_iota(jnp.int32, (NB, NB), 1)).astype(jnp.float32)
    pad = jnp.zeros((NB, 128 - 2 * NB), jnp.float32)
    work = jnp.concatenate([diag, eye, pad], axis=1)
    row = lax.broadcasted_iota(jnp.int32, (NB, 128), 0)
    scale = jnp.zeros((NB, 128), jnp.float32)
    for j in range(0, NB, STEP):
        cols = [jnp.broadcast_to(work[:, j + c:j + c + 1], (NB, 128)) for c in range(STEP)]
        rows = [work[j + c:j + c + 1, :] for c in range(STEP)]
        piv = {(r, c): cols[c][j + r:j + r + 1, :] for r in range(STEP) for c in range(r + 1)}
        for c in range(STEP):
            inv = 1.0 / piv[c, c]
            low = {r: piv[r, c] * inv for r in range(c + 1, STEP)}
            for r in range(c + 1, STEP):
                for q in range(c + 1, r + 1):
                    piv[r, q] = piv[r, q] - low[r] * piv[q, c]
            for r in range(c + 1, STEP):
                rows[r] = rows[r] - low[r] * rows[c]
                cols[r] = cols[r] - low[r] * cols[c]
            scale = jnp.where(row == j + c, inv, scale)
            work = work - jnp.where(row > j + c, cols[c] * inv, 0.0) * rows[c]
    return (work * jnp.sqrt(scale))[:, NB:2 * NB]

def inverse_factor(gram, work):
    n = gram.shape[0]
    eye = (lax.broadcasted_iota(jnp.int32, (n, n), 0) == lax.broadcasted_iota(jnp.int32, (n, n), 1)).astype(jnp.float32)
    work[:, :n] = gram
    work[:, n:] = eye
    for b in range(0, n, NB):
        e = b + NB
        small = factor_block(work[b:e, b:e])
        lo = b // 128 * 128
        hi = n + (e + 127) // 128 * 128
        band = mm(small, work[b:e, lo:hi], ((1,), (0,)))
        work[b:e, lo:hi] = band
        if e < n:
            work[e:, lo:hi] = work[e:, lo:hi] - mm(band[:, e - lo:n - lo], band, ((0,), (0,)))
    return work[:, n:]

def first_kernel(count, packed_ref, start_ref, *refs):
    coords_ref, gram, work = refs[-3:]
    side = start_ref.shape[0] // TILE
    for i in range(side):
        for j in range(i + 1):
            cell = packed_ref[cell_at(i, j):cell_at(i, j) + TILE, :]
            gram[i * TILE:(i + 1) * TILE, j * TILE:(j + 1) * TILE] = cell
            if j < i:
                gram[j * TILE:(j + 1) * TILE, i * TILE:(i + 1) * TILE] = cell.T
    start = start_ref[...].astype(jnp.float32)
    image = mm(gram[...], start, ((1,), (0,)))
    inv_one = inverse_factor(mm(start, image, ((0,), (0,))) * (1 / count), work)
    coords_ref[...] = mm(image, inv_one, ((1,), (1,))) * (1 / count)


def second_kernel(count, gram_ref, coords_ref, *refs):
    mix_ref, work = refs[-2:]
    coords = coords_ref[...]
    image = mm(gram_ref[...], coords, ((1,), (0,)))
    inv_two = inverse_factor(mm(coords, image, ((0,), (0,))) * (1 / count), work)
    mix_ref[...] = mm(coords, inv_two, ((1,), (1,)))


def first_iterate(packed, start, count, after):
    rows = start.shape[0]
    return pl.pallas_call(
        functools.partial(first_kernel, count),
        out_shape=(jax.ShapeDtypeStruct(start.shape, jnp.float32), jax.ShapeDtypeStruct((rows, rows), jnp.float32)),
        in_specs=in_vmem(2) + [pl.BlockSpec(memory_space=pl.ANY)] * len(after),
        out_specs=in_vmem(2),
        scratch_shapes=[pltpu.VMEM((K, 2 * K), jnp.float32)],
        compiler_params=pltpu.CompilerParams(vmem_limit_bytes=12 * MIB),
    )(packed, start, *after)


def second_iterate(gram, coords, count, after):
    return pl.pallas_call(
        functools.partial(second_kernel, count),
        out_shape=jax.ShapeDtypeStruct(coords.shape, jnp.float32),
        in_specs=in_vmem(2) + [pl.BlockSpec(memory_space=pl.ANY)] * len(after),
        out_specs=in_vmem(1)[0],
        scratch_shapes=[pltpu.VMEM((K, 2 * K), jnp.float32)],
        compiler_params=pltpu.CompilerParams(vmem_limit_bytes=12 * MIB),
    )(gram, coords, *after)


def split_kernel(core_ref, private_ref, keep_ref, give_ref, sems):
    depth, _, cols = keep_ref.shape
    copies = []
    for at in range(depth):
        for side, target in enumerate((give_ref, keep_ref)):
            whose = core_ref[0] if side else 1 - core_ref[0]
            start = pl.multiple_of((2 * at + whose) * cols, cols)
            copy = pltpu.make_async_copy(private_ref.at[:, pl.ds(start, cols)], target.at[at], sems.at[2 * at + side])
            copy.start()
            copies.append(copy)
    for copy in copies:
        copy.wait()


def split_by_core(private_grads, cols):
    depth = lax.axis_size("z")
    shape = jax.ShapeDtypeStruct((depth, private_grads.shape[0], cols), jnp.float32)
    return pl.pallas_call(
        split_kernel,
        out_shape=(shape, shape),
        in_specs=[pl.BlockSpec(memory_space=pltpu.SMEM), pl.BlockSpec(memory_space=pltpu.HBM)],
        out_specs=[pl.BlockSpec(memory_space=pltpu.HBM)] * 2,
        scratch_shapes=[pltpu.SemaphoreType.DMA((2 * depth,))],
        compiler_params=pltpu.CompilerParams(vmem_limit_bytes=4 * MIB),
    )(lax.axis_index("core").astype(jnp.int32)[None], private_grads)


def take_kernel(parts, place_ref, *refs):
    held, outs, sems = refs[:len(parts[0])], refs[-len(parts) - 1:-1], refs[-1]
    copies = []
    for at, (part, out_ref) in enumerate(zip(parts, outs)):
        rows = 0
        for which, ref in enumerate(held):
            if part[which]:
                target = out_ref.at[pl.ds(rows, ref.shape[1])]
                copy = pltpu.make_async_copy(ref.at[place_ref[at]], target, sems.at[len(copies)])
                copy.start()
                copies.append(copy)
                rows += ref.shape[1]
    for copy in copies:
        copy.wait()


def take_parts(keep, got, steps, parts, after):
    depth, here = lax.axis_size("z"), lax.axis_index("z")
    local, cols = keep.shape[1:]
    places = jnp.stack([(here + step) % depth for step in steps]).astype(jnp.int32)
    shapes = [jax.ShapeDtypeStruct((sum(part) * local, cols), jnp.float32) for part in parts]
    far, anywhere = pl.BlockSpec(memory_space=pltpu.HBM), pl.BlockSpec(memory_space=pl.ANY)
    return pl.pallas_call(
        functools.partial(take_kernel, parts),
        out_shape=shapes,
        in_specs=[pl.BlockSpec(memory_space=pltpu.SMEM)] + [far] * 2 + [anywhere] * len(after),
        out_specs=[far] * len(parts),
        scratch_shapes=[pltpu.SemaphoreType.DMA((sum(sum(part) for part in parts),))],
        compiler_params=pltpu.CompilerParams(vmem_limit_bytes=4 * MIB),
    )(places, keep, got, *after)


def shift(piece, step):
    depth = lax.axis_size("z")
    return lax.ppermute(piece, "z", [(i, (i + step) % depth) for i in range(depth)])


def row_places(slot, local):
    depth, pair = lax.axis_size("z"), lax.axis_size("core")
    here, core = lax.axis_index("z"), lax.axis_index("core")
    owner = slot // local
    away = (here - owner // pair) % depth
    other = (owner % pair != core).astype(jnp.int32)
    return (away * pair + other) * local + slot % local


def body(public_grads, private_grads, slot, seed_basis):
    total = float(public_grads.shape[1] * lax.axis_size(ALL))
    root = total ** 0.5
    cols = public_grads.shape[1]
    local = private_grads.shape[0]
    plane, depth = lax.axis_size(PLANE), lax.axis_size("z")
    keep, give = split_by_core(private_grads, cols)
    packed = packed_gram(public_grads)
    got = lax.ppermute(give, "core", [(0, 1), (1, 0)])
    whole, own, other = (1, 1), (1, 0), (0, 1)
    early = (whole, whole, whole, other)
    zero, one, seven, relay = take_parts(keep, got, (0, 1, 7, 4), early, [])
    one, seven = shift(one, 1), shift(seven, 7)
    packed = exchange(packed.reshape(plane, -1, TILE), PLANE)
    packed = sum_and_copy(packed, depth, [one, seven])
    relay = shift(relay, 6)
    packed = sum_and_copy(exchange(packed, "z"), plane, [relay])
    steps, parts = (3, 5, 4, 2, 6), (whole, whole, own, whole, whole)
    three, five, four, two, six = take_parts(keep, got, steps, parts, [packed])
    three, five, four, back = shift(three, 3), shift(five, 5), shift(four, 4), shift(relay, 6)
    two, six = shift(two, 2), shift(six, 6)
    packed = exchange(packed, PLANE).reshape(-1, TILE)
    coords, gram = first_iterate(packed, seed_basis, total, [])
    ordered_parts = [zero, one, two, three, four, back, five, six, seven]
    places = row_places(slot, local)[:, None]
    joined, ordered = cross_products(places, public_grads, ordered_parts, coords)
    joined = exchange(joined.reshape(plane, -1, joined.shape[1]), PLANE)
    mix = second_iterate(gram, coords, total, [])
    joined = exchange(sum_and_copy(joined, depth, [mix]), "z")
    held = embed_rows(joined, mix, plane, root)
    held = exchange(held, PLANE).reshape(-1, held.shape[-1])
    basis = lax.dot_general(public_grads, mix, (((0,), (0,)), ((), ())), precision=lax.Precision.HIGH)
    embeddings, squares, close = clip_embeddings(held, root)

    def exact(rough):
        resid = ordered - mm(held[:, :K], basis, ((1,), (1,))) / root
        summed = lax.psum(jnp.sum(resid * resid, axis=1, keepdims=True), ALL)
        return jnp.broadcast_to(summed, rough.shape)

    def quick(rough):
        return rough

    squares = lax.cond(close[0, 0] > 0, exact, quick, squares)
    return (basis, coords, embeddings, scaled_residual(ordered, held, squares, basis, root))


def solution(mesh):
    fine = Mesh(mesh.devices.reshape(4, 4, 8, 2), ALL)
    return jax.shard_map(
        body,
        mesh=fine,
        in_specs=(P(None, ALL), P(("z", "core"), ("x", "y")), P(), P()),
        out_specs=(P(ALL, None), P(), P(), P(None, ALL)),
        check_vma=False,
    )
```

```python
import functools

import jax
import jax.numpy as jnp
from jax import lax
from jax.experimental import pallas as pl
from jax.experimental.pallas import tpu as pltpu
from jax.sharding import Mesh, PartitionSpec as P

K = 256
TILE = 128
NB = 32
STEP = 8
HIGH = lax.Precision.HIGHEST
ALL = ("x", "y", "z", "core")
PLANE = ("x", "y", "core")


def mm(left, right, dims):
    return lax.dot_general(left, right, (dims, ((), ())), precision=HIGH, preferred_element_type=jnp.float32)


MIB = 1024 * 1024


def in_vmem(count):
    return [pl.BlockSpec(memory_space=pltpu.VMEM)] * count


def exchange(pieces, axes):
    return lax.all_to_all(pieces, axes, split_axis=0, concat_axis=0, tiled=True)


def sum_kernel(pieces_ref, *refs):
    out_ref = refs[-1]
    out_ref[...] = jnp.broadcast_to(jnp.sum(pieces_ref[...], axis=0, keepdims=True), out_ref.shape)


def sum_and_copy(pieces, copies, after):
    return pl.pallas_call(
        sum_kernel,
        out_shape=jax.ShapeDtypeStruct((copies,) + pieces.shape[1:], jnp.float32),
        in_specs=in_vmem(1) + [pl.BlockSpec(memory_space=pl.ANY)] * len(after),
        out_specs=in_vmem(1)[0],
        compiler_params=pltpu.CompilerParams(vmem_limit_bytes=8 * MIB),
    )(pieces, *after)


def halves(value):
    high = value.astype(jnp.bfloat16)
    return high, (value - high.astype(jnp.float32)).astype(jnp.bfloat16)


def dot_low(left, right, dims):
    return lax.dot_general(left, right, (dims, ((), ())), preferred_element_type=jnp.float32)


def mm_halves(left, right, dims):
    small = dot_low(left[0], right[1], dims) + dot_low(left[1], right[0], dims)
    return dot_low(left[0], right[0], dims) + small


def cell_at(i, j):
    return (i * (i + 1) // 2 + j) * TILE


def gram_kernel(grads_ref, packed_ref):
    rows = grads_ref.shape[0]
    band = 2 * TILE
    first = pl.program_id(0) == 0
    high, low = halves(grads_ref[...])
    for top in range(0, rows, band):
        end = top + band
        part = mm_halves((high[top:end], low[top:end]), (high[:end], low[:end]), ((1,), (1,)))
        for i in (top // TILE, top // TILE + 1):
            for j in range(i + 1):
                at = cell_at(i, j)
                cell = part[i * TILE - top:(i + 1) * TILE - top, j * TILE:(j + 1) * TILE]
                packed_ref[at:at + TILE, :] = cell + jnp.where(first, 0.0, packed_ref[at:at + TILE, :])


def packed_gram(grads):
    rows, cols = grads.shape
    side = rows // TILE
    chunk = 512
    return pl.pallas_call(
        gram_kernel,
        grid=(cols // chunk,),
        out_shape=jax.ShapeDtypeStruct((side * (side + 1) // 2 * TILE, TILE), jnp.float32),
        in_specs=[pl.BlockSpec((rows, chunk), lambda i: (0, i))],
        out_specs=pl.BlockSpec((side * (side + 1) // 2 * TILE, TILE), lambda i: (0, 0)),
        compiler_params=pltpu.CompilerParams(vmem_limit_bytes=12 * MIB),
    )(grads)


def cross_kernel(parts, index_ref, *refs):
    held, (joined_ref, ordered_ref, rows_ref, grads, sems) = refs[:parts + 1], refs[-5:]
    copies, at = [], 0
    for piece in held[:parts]:
        copies.append(pltpu.make_async_copy(piece, rows_ref.at[pl.ds(at, piece.shape[0])], sems.at[len(copies)]))
        at += piece.shape[0]
    copies.append(pltpu.make_async_copy(held[parts], grads, sems.at[parts]))
    for copy in copies:
        copy.start()
    for copy in copies[:parts]:
        copy.wait()
    rows = grads.shape[0]
    values = rows_ref[...]
    count = values.shape[0]
    pick = (index_ref[...] == lax.broadcasted_iota(jnp.int32, (count, count), 1)).astype(jnp.bfloat16)
    high = values.astype(jnp.bfloat16)
    rest = values - high.astype(jnp.float32)
    middle = rest.astype(jnp.bfloat16)
    low = (rest - middle.astype(jnp.float32)).astype(jnp.bfloat16)
    high, middle, low = [dot_low(pick, piece, ((1,), (0,))) for piece in (high, middle, low)]
    ordered = (high + middle) + low
    ordered_ref[...] = ordered
    norms = jnp.sum(ordered * ordered, axis=1, keepdims=True)
    joined_ref[:, rows:] = jnp.broadcast_to(norms, (count, TILE))
    left = (high.astype(jnp.bfloat16), middle.astype(jnp.bfloat16))
    copies[parts].wait()
    joined_ref[:, :rows] = mm_halves(left, halves(grads[...]), ((1,), (1,)))


def cross_products(index, grads, pieces, after):
    count = sum(piece.shape[0] for piece in pieces)
    rows, cols = grads.shape
    far = pl.BlockSpec(memory_space=pltpu.HBM)
    return pl.pallas_call(
        functools.partial(cross_kernel, len(pieces)),
        out_shape=(jax.ShapeDtypeStruct((count, rows + TILE), jnp.float32), jax.ShapeDtypeStruct((count, cols), jnp.float32)),
        in_specs=in_vmem(1) + [far] * (1 + len(pieces)) + [pl.BlockSpec(memory_space=pl.ANY)],
        out_specs=in_vmem(2),
        scratch_shapes=[
            pltpu.VMEM((count, cols), jnp.float32),
            pltpu.VMEM((rows, cols), jnp.float32),
            pltpu.SemaphoreType.DMA((len(pieces) + 1,)),
        ],
        compiler_params=pltpu.CompilerParams(vmem_limit_bytes=26 * MIB),
    )(index, *pieces, grads, after)


def rows_kernel(root, joined_ref, mix_ref, out_ref):
    rows = mix_ref.shape[0]
    joined = jnp.sum(joined_ref[...], axis=0)
    embed = mm(joined[:, :rows], mix_ref[...], ((1,), (0,))) * (1 / root)
    held = jnp.concatenate([embed, joined[:, rows:]], axis=1)
    out_ref[...] = jnp.broadcast_to(held[None], out_ref.shape)


def embed_rows(joined, mix, copies, root):
    return pl.pallas_call(
        functools.partial(rows_kernel, root),
        out_shape=jax.ShapeDtypeStruct((copies, joined.shape[1], K + TILE), jnp.float32),
        in_specs=in_vmem(2),
        out_specs=in_vmem(1)[0],
        compiler_params=pltpu.CompilerParams(vmem_limit_bytes=8 * MIB),
    )(joined, mix)


def clip_kernel(root, held_ref, embed_ref, squares_ref, close_ref):
    embed = held_ref[:, :K]
    norms = held_ref[:, K:]
    squares = jnp.sum(embed * embed, axis=1, keepdims=True)
    embed_ref[...] = embed * jnp.minimum(1.0, 1.5 * K ** 0.5 / jnp.sqrt(squares + 1e-06))
    rough = jnp.maximum(norms - squares, 0.0)
    squares_ref[...] = rough
    close = (rough < 0.05 * norms) & (norms > 2.25 * root * root)
    close_ref[0, 0] = jnp.max(close.astype(jnp.int32))


def clip_embeddings(held, root):
    count = held.shape[0]
    return pl.pallas_call(
        functools.partial(clip_kernel, root),
        out_shape=(
            jax.ShapeDtypeStruct((count, K), jnp.float32),
            jax.ShapeDtypeStruct((count, TILE), jnp.float32),
            jax.ShapeDtypeStruct((1, 1), jnp.int32),
        ),
        in_specs=in_vmem(1),
        out_specs=in_vmem(2) + [pl.BlockSpec(memory_space=pltpu.SMEM)],
        compiler_params=pltpu.CompilerParams(vmem_limit_bytes=8 * MIB),
    )(held)


def final_kernel(root, ordered_ref, held_ref, squares_ref, basis_ref, out_ref):
    projected = mm_halves(halves(held_ref[:, :K]), halves(basis_ref[...]), ((1,), (1,)))
    scale = jnp.minimum(1.0, 1.5 * root / jnp.sqrt(squares_ref[:, :1] + 1e-06))
    out_ref[...] = (ordered_ref[...] - projected * (1 / root)) * scale


def scaled_residual(ordered, held, squares, basis, root):
    count, cols = ordered.shape
    chunk = 512
    return pl.pallas_call(
        functools.partial(final_kernel, root),
        grid=(cols // chunk,),
        out_shape=jax.ShapeDtypeStruct((count, cols), jnp.float32),
        in_specs=[
            pl.BlockSpec((count, chunk), lambda i: (0, i)),
            pl.BlockSpec((count, K + TILE), lambda i: (0, 0)),
            pl.BlockSpec((count, TILE), lambda i: (0, 0)),
            pl.BlockSpec((chunk, K), lambda i: (i, 0)),
        ],
        out_specs=pl.BlockSpec((count, chunk), lambda i: (0, i)),
        compiler_params=pltpu.CompilerParams(vmem_limit_bytes=12 * MIB),
    )(ordered, held, squares, basis)


def factor_block(diag):
    eye = (lax.broadcasted_iota(jnp.int32, (NB, NB), 0) == lax.broadcasted_iota(jnp.int32, (NB, NB), 1)).astype(jnp.float32)
    pad = jnp.zeros((NB, 128 - 2 * NB), jnp.float32)
    work = jnp.concatenate([diag, eye, pad], axis=1)
    row = lax.broadcasted_iota(jnp.int32, (NB, 128), 0)
    scale = jnp.zeros((NB, 128), jnp.float32)
    for j in range(0, NB, STEP):
        cols = [jnp.broadcast_to(work[:, j + c:j + c + 1], (NB, 128)) for c in range(STEP)]
        rows = [work[j + c:j + c + 1, :] for c in range(STEP)]
        piv = {(r, c): cols[c][j + r:j + r + 1, :] for r in range(STEP) for c in range(r + 1)}
        for c in range(STEP):
            inv = 1.0 / piv[c, c]
            low = {r: piv[r, c] * inv for r in range(c + 1, STEP)}
            for r in range(c + 1, STEP):
                for q in range(c + 1, r + 1):
                    piv[r, q] = piv[r, q] - low[r] * piv[q, c]
            for r in range(c + 1, STEP):
                rows[r] = rows[r] - low[r] * rows[c]
                cols[r] = cols[r] - low[r] * cols[c]
            scale = jnp.where(row == j + c, inv, scale)
            work = work - jnp.where(row > j + c, cols[c] * inv, 0.0) * rows[c]
    return (work * jnp.sqrt(scale))[:, NB:2 * NB]

def inverse_factor(gram, work):
    n = gram.shape[0]
    eye = (lax.broadcasted_iota(jnp.int32, (n, n), 0) == lax.broadcasted_iota(jnp.int32, (n, n), 1)).astype(jnp.float32)
    work[:, :n] = gram
    work[:, n:] = eye
    for b in range(0, n, NB):
        e = b + NB
        small = factor_block(work[b:e, b:e])
        lo = b // 128 * 128
        hi = n + (e + 127) // 128 * 128
        band = mm(small, work[b:e, lo:hi], ((1,), (0,)))
        work[b:e, lo:hi] = band
        if e < n:
            work[e:, lo:hi] = work[e:, lo:hi] - mm(band[:, e - lo:n - lo], band, ((0,), (0,)))
    return work[:, n:]

def first_kernel(count, packed_ref, start_ref, *refs):
    coords_ref, gram, token_ref, work = refs[-4:]
    token_ref[...] = jnp.zeros_like(token_ref)
    side = start_ref.shape[0] // TILE
    for i in range(side):
        for j in range(i + 1):
            cell = packed_ref[cell_at(i, j):cell_at(i, j) + TILE, :]
            gram[i * TILE:(i + 1) * TILE, j * TILE:(j + 1) * TILE] = cell
            if j < i:
                gram[j * TILE:(j + 1) * TILE, i * TILE:(i + 1) * TILE] = cell.T
    start = start_ref[...].astype(jnp.float32)
    image = mm(gram[...], start, ((1,), (0,)))
    inv_one = inverse_factor(mm(start, image, ((0,), (0,))) * (1 / count), work)
    coords_ref[...] = mm(image, inv_one, ((1,), (1,))) * (1 / count)


def second_kernel(count, gram_ref, coords_ref, *refs):
    mix_ref, work = refs[-2:]
    coords = coords_ref[...]
    image = mm(gram_ref[...], coords, ((1,), (0,)))
    inv_two = inverse_factor(mm(coords, image, ((0,), (0,))) * (1 / count), work)
    mix_ref[...] = mm(coords, inv_two, ((1,), (1,)))


def first_iterate(packed, start, count, after):
    rows = start.shape[0]
    token = jax.ShapeDtypeStruct((8, TILE), jnp.float32)
    return pl.pallas_call(
        functools.partial(first_kernel, count),
        out_shape=(jax.ShapeDtypeStruct(start.shape, jnp.float32), jax.ShapeDtypeStruct((rows, rows), jnp.float32), token),
        in_specs=in_vmem(2) + [pl.BlockSpec(memory_space=pl.ANY)] * len(after),
        out_specs=in_vmem(3),
        scratch_shapes=[pltpu.VMEM((K, 2 * K), jnp.float32)],
        compiler_params=pltpu.CompilerParams(vmem_limit_bytes=12 * MIB),
    )(packed, start, *after)


def second_iterate(gram, coords, count, after):
    return pl.pallas_call(
        functools.partial(second_kernel, count),
        out_shape=jax.ShapeDtypeStruct(coords.shape, jnp.float32),
        in_specs=in_vmem(2) + [pl.BlockSpec(memory_space=pl.ANY)] * len(after),
        out_specs=in_vmem(1)[0],
        scratch_shapes=[pltpu.VMEM((K, 2 * K), jnp.float32)],
        compiler_params=pltpu.CompilerParams(vmem_limit_bytes=12 * MIB),
    )(gram, coords, *after)


def split_kernel(core_ref, private_ref, keep_ref, give_ref, sems):
    depth, _, cols = keep_ref.shape
    copies = []
    for at in range(depth):
        for side, target in enumerate((give_ref, keep_ref)):
            whose = core_ref[0] if side else 1 - core_ref[0]
            start = pl.multiple_of((2 * at + whose) * cols, cols)
            copy = pltpu.make_async_copy(private_ref.at[:, pl.ds(start, cols)], target.at[at], sems.at[2 * at + side])
            copy.start()
            copies.append(copy)
    for copy in copies:
        copy.wait()


def split_by_core(private_grads, cols):
    depth = lax.axis_size("z")
    shape = jax.ShapeDtypeStruct((depth, private_grads.shape[0], cols), jnp.float32)
    return pl.pallas_call(
        split_kernel,
        out_shape=(shape, shape),
        in_specs=[pl.BlockSpec(memory_space=pltpu.SMEM), pl.BlockSpec(memory_space=pltpu.HBM)],
        out_specs=[pl.BlockSpec(memory_space=pltpu.HBM)] * 2,
        scratch_shapes=[pltpu.SemaphoreType.DMA((2 * depth,))],
        compiler_params=pltpu.CompilerParams(vmem_limit_bytes=4 * MIB),
    )(lax.axis_index("core").astype(jnp.int32)[None], private_grads)


def take_kernel(parts, place_ref, *refs):
    held, outs, sems = refs[:len(parts[0])], refs[-len(parts) - 1:-1], refs[-1]
    copies = []
    for at, (part, out_ref) in enumerate(zip(parts, outs)):
        rows = 0
        for which, ref in enumerate(held):
            if part[which]:
                target = out_ref.at[pl.ds(rows, ref.shape[1])]
                copy = pltpu.make_async_copy(ref.at[place_ref[at]], target, sems.at[len(copies)])
                copy.start()
                copies.append(copy)
                rows += ref.shape[1]
    for copy in copies:
        copy.wait()


def take_parts(keep, got, steps, parts, after):
    depth, here = lax.axis_size("z"), lax.axis_index("z")
    local, cols = keep.shape[1:]
    places = jnp.stack([(here + step) % depth for step in steps]).astype(jnp.int32)
    shapes = [jax.ShapeDtypeStruct((sum(part) * local, cols), jnp.float32) for part in parts]
    far, anywhere = pl.BlockSpec(memory_space=pltpu.HBM), pl.BlockSpec(memory_space=pl.ANY)
    return pl.pallas_call(
        functools.partial(take_kernel, parts),
        out_shape=shapes,
        in_specs=[pl.BlockSpec(memory_space=pltpu.SMEM)] + [far] * 2 + [anywhere] * len(after),
        out_specs=[far] * len(parts),
        scratch_shapes=[pltpu.SemaphoreType.DMA((sum(sum(part) for part in parts),))],
        compiler_params=pltpu.CompilerParams(vmem_limit_bytes=4 * MIB),
    )(places, keep, got, *after)


def shift(piece, step):
    depth = lax.axis_size("z")
    return lax.ppermute(piece, "z", [(i, (i + step) % depth) for i in range(depth)])


def row_places(slot, local):
    depth, pair = lax.axis_size("z"), lax.axis_size("core")
    here, core = lax.axis_index("z"), lax.axis_index("core")
    owner = slot // local
    away = (here - owner // pair) % depth
    other = (owner % pair != core).astype(jnp.int32)
    return (away * pair + other) * local + slot % local


def body(public_grads, private_grads, slot, seed_basis):
    total = float(public_grads.shape[1] * lax.axis_size(ALL))
    root = total ** 0.5
    cols = public_grads.shape[1]
    local = private_grads.shape[0]
    plane, depth = lax.axis_size(PLANE), lax.axis_size("z")
    keep, give = split_by_core(private_grads, cols)
    packed = packed_gram(public_grads)
    got = lax.ppermute(give, "core", [(0, 1), (1, 0)])
    whole, own, other = (1, 1), (1, 0), (0, 1)
    early = (whole, whole, whole, other, own)
    zero, one, seven, relay, four = take_parts(keep, got, (0, 1, 7, 4, 4), early, [])
    one, seven = shift(one, 1), shift(seven, 7)
    packed = exchange(packed.reshape(plane, -1, TILE), PLANE)
    packed = sum_and_copy(packed, depth, [one, seven])
    relay = shift(relay, 6)
    packed = sum_and_copy(exchange(packed, "z"), plane, [relay])
    three, five, two, six = take_parts(keep, got, (3, 5, 2, 6), (whole,) * 4, [packed])
    three, five, four, back = shift(three, 3), shift(five, 5), shift(four, 4), shift(relay, 6)
    two, six = shift(two, 2), shift(six, 6)
    packed = exchange(packed, PLANE).reshape(-1, TILE)
    coords, gram, done = first_iterate(packed, seed_basis, total, [])
    ordered_parts = [zero, one, two, three, four, back, five, six, seven]
    places = row_places(slot, local)[:, None]
    joined, ordered = cross_products(places, public_grads, ordered_parts, done)
    joined = exchange(joined.reshape(plane, -1, joined.shape[1]), PLANE)
    mix = second_iterate(gram, coords, total, [])
    joined = exchange(sum_and_copy(joined, depth, [mix]), "z")
    held = embed_rows(joined, mix, plane, root)
    held = exchange(held, PLANE).reshape(-1, held.shape[-1])
    basis = lax.dot_general(public_grads, mix, (((0,), (0,)), ((), ())), precision=lax.Precision.HIGH)
    embeddings, squares, close = clip_embeddings(held, root)

    def exact(rough):
        resid = ordered - mm(held[:, :K], basis, ((1,), (1,))) / root
        summed = lax.psum(jnp.sum(resid * resid, axis=1, keepdims=True), ALL)
        return jnp.broadcast_to(summed, rough.shape)

    def quick(rough):
        return rough

    squares = lax.cond(close[0, 0] > 0, exact, quick, squares)
    return (basis, coords, embeddings, scaled_residual(ordered, held, squares, basis, root))


def solution(mesh):
    fine = Mesh(mesh.devices.reshape(4, 4, 8, 2), ALL)
    return jax.shard_map(
        body,
        mesh=fine,
        in_specs=(P(None, ALL), P(("z", "core"), ("x", "y")), P(), P()),
        out_specs=(P(ALL, None), P(), P(), P(None, ALL)),
        check_vma=False,
    )
```
